256 devices in a mesh: fsdp: 16 (over y_lo, x, core), seq: 16 (over y_hi, z).
Axes of the slice: x: 4, y: 4 (y_hi: 2, y_lo: 2; y = y_hi * 2 + y_lo), z: 8, core: 2. Of those that a mesh axis runs over, the one named last changes fastest.
Arguments:
- primal: bfloat16 [4096, 5120], P('seq', 'fsdp'), may hold values from -6 to 6
- tangent: bfloat16 [4096, 5120], P('seq', 'fsdp'), may hold values from -6 to 6
- w_in: bfloat16 [5120, 13824], P('seq', 'fsdp'), may hold values from -0.078125 to 0.078125
- b_in: float32 [13824], P('fsdp'), may hold values from -3 to 3
- w_out: bfloat16 [13824, 5120], P('fsdp', 'seq'), may hold values from -0.0625 to 0.0625
- b_out: float32 [5120], replicated, may hold values from -3 to 3
- gate_mod: float32 [5120], replicated, may hold values from 0.5 to 1.5
- gate_tan: float32 [5120], replicated, may hold values from -3 to 3
Outputs:
- branch_out: bfloat16 [16, 256, 5120], P(None, 'fsdp', 'seq')
- branch_tan: bfloat16 [16, 256, 5120], P(None, 'fsdp', 'seq')
The draws below stay inside these ranges and needn't reach their ends.
All inputs are finite; a program needn't handle non-finite values.
Results may differ from the reference program's by a relative error of at most 0.024.
Values may be sent and summed in bfloat16 or wider, within the bound.
A program may use at most 64 MiB of HBM per device.

```python
import jax
import jax.numpy as jnp
from jax import lax

D = 5120
FF = 13824
TOK_DEV = 256
TOKENS = 4096
N_FSDP = 16
N_SEQ = 16


def with_spikes(entries, stream_key, source, target, blocks, factor):
    def block_of(position):
        return (jnp.arange(entries.shape[position]) // (entries.shape[position] // blocks)).reshape((-1,) + (1,) * (entries.ndim - 1 - position))

    near = jax.random.permutation(stream_key, blocks)[block_of(target)]
    other_side = (block_of(target) + blocks // 2) % blocks
    return jnp.where((block_of(source) == near) | (block_of(source) == other_side), factor * entries, entries)


def block_scale(stream_key, shape, shards, low, high):
    def one(position, parts):
        draws = jax.random.uniform(jax.random.fold_in(jax.random.fold_in(stream_key, 6), position), (parts,), jnp.float32, low / len(shards), high / len(shards))
        return jnp.repeat(jnp.exp(draws), shape[position] // parts).reshape((-1,) + (1,) * (len(shape) - position - 1))

    level = one(*shards[0])
    for cut in shards[1:]:
        level = level * one(*cut)
    return level


def bell_draw(rng, shape, spread, reach, split=(), kind=jnp.bfloat16):
    gain = block_scale(rng, shape, split, -0.22, 0.18) if split else 1.0
    entries = jax.random.normal(rng, shape, jnp.float32) * spread * gain
    return jnp.minimum(jnp.maximum(entries, -reach), reach).astype(kind)


def bell_draw_with(key, extent, deviation, most, shards, heavy, held_as=jnp.bfloat16):
    values = deviation * jax.random.normal(key, extent, jnp.float32)
    if shards:
        values = values * block_scale(key, extent, shards, -0.22, 0.18)
    return jnp.clip(with_spikes(values, jax.random.fold_in(key, 3), *heavy), -most, most).astype(held_as)


def setup_inputs(seed: int = 0) -> dict:
    key_of = jax.random.split(jax.random.key(seed), 9)
    return {
        "primal": bell_draw(key_of[0], (TOKENS, D), 1.0, 6.0, ((0, 16), (1, 16))),
        "tangent": bell_draw(key_of[1], (TOKENS, D), 1.0, 6.0, ((0, 16), (1, 16))),
        "w_in": bell_draw(key_of[2], (D, FF), D ** -0.5, 0.078125, ((0, 16), (1, 16))),
        "b_in": bell_draw(key_of[3], (FF,), 0.5, 3.0, ((0, 16),), jnp.float32),
        "w_out": bell_draw_with(key_of[4], (FF, D), FF ** -0.5, 0.0625, ((0, 16), (1, 16)), (0, 1, 16, 2.0)),
        "b_out": bell_draw(key_of[5], (D,), 0.5, 3.0, (), jnp.float32),
        "gate_mod": jnp.clip(jax.random.uniform(key_of[6], (D,), jnp.float32, 0.5, 1.5), 0.5, 1.5),
        "gate_tan": bell_draw(key_of[7], (D,), 0.5, 3.0, (), jnp.float32),
    }


def gelu_pair(pre):
    inner = 0.7978845608 * (pre + 0.044715 * pre * pre * pre)
    curve = jnp.tanh(inner)
    value = 0.5 * pre * (1.0 + curve)
    slope = 0.5 * (1.0 + curve) + 0.5 * pre * (1.0 - curve * curve) * 0.7978845608 * (1.0 + 3.0 * 0.044715 * pre * pre)
    return value, slope


def reference(primal, tangent, w_in, b_in, w_out, b_out, gate_mod, gate_tan):
    pre = jnp.dot(primal, w_in, preferred_element_type=jnp.float32) + b_in
    pre_tan = jnp.dot(tangent, w_in, preferred_element_type=jnp.float32)
    value, slope = gelu_pair(pre)
    hidden = value.astype(jnp.bfloat16)
    hidden_tan = (slope * pre_tan).astype(jnp.bfloat16)
    width = FF // N_FSDP

    def add_block(carry, index):
        offset = (index * width).astype(jnp.int32)
        cols = lax.dynamic_slice_in_dim(hidden, offset, width, 1)
        cols_tan = lax.dynamic_slice_in_dim(hidden_tan, offset, width, 1)
        rows_w = lax.dynamic_slice_in_dim(w_out, offset, width, 0)
        part = jnp.dot(cols, rows_w, preferred_element_type=jnp.float32).astype(jnp.bfloat16)
        part_tan = jnp.dot(cols_tan, rows_w, preferred_element_type=jnp.float32).astype(jnp.bfloat16)
        part, part_tan = lax.optimization_barrier((part, part_tan))
        return (carry[0] + part.astype(jnp.float32), carry[1] + part_tan.astype(jnp.float32)), None

    zeros = jnp.zeros((primal.shape[0], w_out.shape[1]), jnp.float32)
    (total, total_tan), unused = lax.scan(add_block, (zeros, zeros), jnp.arange(N_FSDP, dtype=jnp.int32))
    shifted = total + b_out
    out_full = (gate_mod * shifted).astype(jnp.bfloat16)
    tan_full = (gate_mod * total_tan + gate_tan * shifted).astype(jnp.bfloat16)
    return out_full.reshape(N_SEQ, TOK_DEV, D), tan_full.reshape(N_SEQ, TOK_DEV, D)
```

```python
import functools

import jax
import jax.numpy as jnp
from jax import lax
from jax.experimental import pallas as pl
from jax.experimental.pallas import tpu as pltpu
from jax.sharding import PartitionSpec as P

MESH = pl.DeviceIdType.MESH
ORDER = (0, 1, 7, 2, 6, 3, 5, 4)


def gelu_pair(pre):
    inner = 0.7978845608 * (pre + 0.044715 * pre * pre * pre)
    curve = jnp.tanh(inner)
    value = 0.5 * pre * (1.0 + curve)
    slope = 0.5 * (1.0 + curve) + 0.5 * pre * (1.0 - curve * curve) * 0.7978845608 * (
        1.0 + 3.0 * 0.044715 * pre * pre
    )
    return value, slope


def reach(q, way):
    return 4 if (q == 0) == (way == 1) else 3


def kernel(
    x_in, w_in, b_in, gates,
    out_p, out_t,
    wbuf, xbuf, bias, acc, hid, part, r1x, r1y, s2x, s2y, r2x, r2y, fin, land,
    swap_s, swap_r, bias_s, bias_r, ring_s, ring_r, sib_s, sib_r,
    xs1_s, xs1_r, xs2_s, xs2_r, rs1_s, rs1_r, rs2_s, rs2_r, fin_s, fin_r,
):
    f = lax.axis_index("fsdp")
    s = lax.axis_index("seq")
    core = lax.rem(f, 2)
    x = lax.rem(f // 2, 4)
    y_lo = f // 8
    y_hi = s // 8
    z = lax.rem(s, 8)
    y = y_hi * 2 + y_lo
    sends = []

    def dev(xx, yy, zz, cc):
        return (lax.rem(yy, 2) * 8 + xx * 2 + cc, (yy // 2) * 8 + zz)

    def at(dx=0, dy=0, dz=0, flip=False):
        return dev(
            lax.rem(x + dx + 4, 4), lax.rem(y + dy + 4, 4), lax.rem(z + dz + 8, 8),
            1 - core if flip else core,
        )

    def copy(src, dst, ssem, rsem, where):
        return pltpu.make_async_remote_copy(
            src_ref=src, dst_ref=dst, send_sem=ssem, recv_sem=rsem, device_id=where, device_id_type=MESH
        )

    def send(src, dst, ssem, rsem, where):
        c = copy(src, dst, ssem, rsem, where)
        c.start()
        sends.append(c)

    def arrived(dst, ssem, rsem, where):
        copy(dst, dst, ssem, rsem, where).wait_recv()

    barrier = pltpu.get_barrier_semaphore()
    friends = [at(dz=d, flip=fl) for d in range(8) for fl in (False, True) if d or fl]
    friends += [at(dx=d) for d in (1, 2, 3)] + [at(dy=d) for d in (1, 2, 3)] + [at(dy=2, flip=True)]
    for who in friends:
        pl.semaphore_signal(barrier, inc=1, device_id=who, device_id_type=MESH)
    pl.semaphore_wait(barrier, len(friends))

    me_k = (y_lo * 4 + x) * 2 + y_hi
    rows = lambda q: pl.ds(q * 160, 160)
    half = lambda a: pl.ds(a * 128, 128)
    stays = y_hi == core
    partner = at(dy=2, flip=True)
    pieces = []
    for h in range(2):
        for q in range(2):
            pieces.append((w_in.at[h, rows(q)], wbuf.at[h, 0, core, rows(q)], wbuf.at[h, 0, 1 - core, rows(q)]))
    other_k = (y_lo * 4 + x) * 2 + core
    xp = [(x_in.at[half(a)], xbuf.at[me_k, half(a)], xbuf.at[(y_lo * 4 + x) * 2 + 1 - y_hi, half(a)]) for a in range(2)]
    pieces = [pieces[0], pieces[1], xp[0], xp[1], pieces[2], pieces[3]]

    @pl.when(stays)
    def _():
        for i, (src, dst, _away) in enumerate(pieces):
            pltpu.make_async_copy(src, dst, swap_r.at[i]).start()

    @pl.when(jnp.logical_not(stays))
    def _():
        for i, (src, _dst, away) in enumerate(pieces):
            copy(src, away, swap_s.at[i], swap_r.at[i], partner).start()

    send(b_in, bias.at[core], bias_s, bias_r, at(flip=True))
    bias[core] = b_in[...]

    def own(i):
        src, dst, _ = pieces[i]
        pltpu.make_async_copy(src, dst, swap_r.at[i]).wait()

    def w_at(h, delta, q, who=None):
        return wbuf.at[h, delta % 8, core if who is None else who, rows(q)]

    def ring_send(h, q, way, d):
        send(
            w_at(h, -way * (d - 1), q), w_at(h, -way * d, q),
            ring_s.at[h, q, (way + 1) // 2, d - 1], ring_r.at[h, q, (way + 1) // 2, d - 1], at(dz=way),
        )

    def sib_send(h, q, delta):
        send(w_at(h, delta, q), w_at(h, delta, q), sib_s.at[h, q, delta % 8], sib_r.at[h, q, delta % 8], at(flip=True))

    def sib_wait(h, delta):
        for q in range(2):
            arrived(w_at(h, delta, q, 1 - core), sib_s.at[h, q, delta % 8], sib_r.at[h, q, delta % 8], at(flip=True))

    def ring_step(h, d):
        for q in range(2):
            for way in (1, -1):
                if d > reach(q, way):
                    continue
                arrived(
                    w_at(h, -way * d, q),
                    ring_s.at[h, q, (way + 1) // 2, d - 1], ring_r.at[h, q, (way + 1) // 2, d - 1], at(dz=way),
                )
                if d < reach(q, way):
                    ring_send(h, q, way, d + 1)
                sib_send(h, q, -way * d)

    def ring_open(h, q, i):
        own(i)
        for way in (1, -1):
            ring_send(h, q, way, 1)
        sib_send(h, q, 0)

    def x_slot(a, dx, dy):
        xx, yy = lax.rem(x + dx + 8, 4), lax.rem(y + dy + 8, 4)
        return xbuf.at[(lax.rem(yy, 2) * 4 + xx) * 2 + yy // 2, half(a)]

    def x_first(a, d):
        return (d, 0) if a == 0 else (0, d)

    ring_open(0, 0, 0)
    ring_open(0, 1, 1)
    for a in range(2):
        own(2 + a)
        for d in (1, 2, 3):
            dx, dy = x_first(a, d)
            send(x_slot(a, 0, 0), x_slot(a, 0, 0), xs1_s.at[a, d - 1], xs1_r.at[a, d - 1], at(dx, dy))
    acc[...] = jnp.zeros_like(acc)
    own(4)
    own(5)

    def x_second(a, r, d):
        dx, dy = x_first(1 - a, d)
        sx, sy = x_first(a, -r)
        send(x_slot(a, sx, sy), x_slot(a, sx, sy), xs2_s.at[a, r, d - 1], xs2_r.at[a, r, d - 1], at(dx, dy))

    def x_arrive(a, r):
        for d in (1, 2, 3):
            dx, dy = x_first(1 - a, -d)
            sx, sy = x_first(a, -r)
            arrived(x_slot(a, dx + sx, dy + sy), xs2_s.at[a, r, d - 1], xs2_r.at[a, r, d - 1], at(dx, dy))

    for a in range(2):
        for d in (1, 2, 3):
            x_second(a, 0, d)
    ring_step(0, 1)
    for r in (1, 3, 2):
        for a in range(2):
            sx, sy = x_first(a, -r)
            arrived(x_slot(a, sx, sy), xs1_s.at[a, r - 1], xs1_r.at[a, r - 1], at(sx, sy))
            for d in (1, 2, 3):
                x_second(a, r, d)
    ring_step(0, 2)
    ring_step(0, 3)
    for q in range(2):
        for way in (1, -1):
            ring_send(1, q, way, 1)
        sib_send(1, q, 0)
    ring_step(0, 4)
    for a in range(2):
        for r in range(4):
            x_arrive(a, r)
    for delta in ORDER:
        sib_wait(0, delta)
    arrived(bias.at[1 - core], bias_s, bias_r, at(flip=True))

    def first(i, carry):
        delta, h = i // 2, lax.rem(i, 2)
        k = h * 8 + lax.rem(z + delta, 8)
        w = wbuf[0, delta, h]
        xk = xbuf[k]
        acc[0] += jnp.dot(xk[:, :320], w, preferred_element_type=jnp.float32)
        acc[1] += jnp.dot(xk[:, 320:], w, preferred_element_type=jnp.float32)
        return carry

    lax.fori_loop(0, 16, first, 0)

    def activate(i, carry):
        r = pl.ds(pl.multiple_of(i * 32, 32), 32)
        into = pl.ds(pl.multiple_of(lax.rem(i, 4) * 32, 32), 32)
        value, slope = gelu_pair(acc[0, r, :] + bias[y_hi])
        hid[i // 4, 0, into, :] = value.astype(jnp.bfloat16)
        hid[i // 4, 1, into, :] = (slope * acc[1, r, :]).astype(jnp.bfloat16)
        return carry

    lax.fori_loop(0, 8, activate, 0)

    def second(i):
        delta = ORDER[i]

        def body(j, carry):
            h, yl = j // 2, lax.rem(j, 2)
            both = lax.dot_general(
                hid[yl].reshape(256, 864), wbuf[1, delta, h], (((1,), (1,)), ((), ())),
                preferred_element_type=jnp.float32,
            )
            packed = jnp.concatenate([both[:128], both[128:]], axis=1).astype(jnp.bfloat16)
            for b in range(8):
                part[i, b % 2, h, yl, b // 2] = packed[b * 16 : (b + 1) * 16]
            return carry

        lax.fori_loop(0, 4, body, 0)
        for d in (1, 2, 3):
            xx = lax.rem(x + d, 4)
            send(part.at[i, 0, :, :, xx], r1x.at[i, d - 1], rs1_s.at[i, 0, d - 1], rs1_r.at[i, 0, d - 1], at(dx=d))
            yy = lax.rem(y + d, 4)
            send(
                part.at[i, 1, yy // 2, lax.rem(yy, 2)], r1y.at[i, d - 1],
                rs1_s.at[i, 1, d - 1], rs1_r.at[i, 1, d - 1], at(dy=d),
            )

    f32 = lambda v: v.astype(jnp.float32)

    def reduce_one(i):
        for d in (1, 2, 3):
            arrived(r1x.at[i, d - 1], rs1_s.at[i, 0, d - 1], rs1_r.at[i, 0, d - 1], at(dx=-d))
        for h in range(2):
            for yl in range(2):
                t = f32(part[i, 0, h, yl, x])
                for d in range(3):
                    t += f32(r1x[i, d, h, yl])
                s2x[i, h, yl] = t.astype(jnp.bfloat16)
        for d in (1, 2, 3):
            yy = lax.rem(y + d, 4)
            send(
                s2x.at[i, yy // 2, lax.rem(yy, 2)], r2x.at[i, d - 1],
                rs2_s.at[i, 0, d - 1], rs2_r.at[i, 0, d - 1], at(dy=d),
            )
        for d in (1, 2, 3):
            arrived(r1y.at[i, d - 1], rs1_s.at[i, 1, d - 1], rs1_r.at[i, 1, d - 1], at(dy=-d))
        for b in range(4):
            t = f32(part[i, 1, y_hi, y_lo, b])
            for d in range(3):
                t += f32(r1y[i, d, b])
            s2y[i, b] = t.astype(jnp.bfloat16)
        for d in (1, 2, 3):
            send(s2y.at[i, lax.rem(x + d, 4)], r2y.at[i, d - 1], rs2_s.at[i, 1, d - 1], rs2_r.at[i, 1, d - 1], at(dx=d))

    def reduce_two(i):
        delta = ORDER[i]
        g = gates[y_hi * 8 + lax.rem(z + delta, 8)]
        for d in (1, 2, 3):
            arrived(r2x.at[i, d - 1], rs2_s.at[i, 0, d - 1], rs2_r.at[i, 0, d - 1], at(dy=-d))
            arrived(r2y.at[i, d - 1], rs2_s.at[i, 1, d - 1], rs2_r.at[i, 1, d - 1], at(dx=-d))
        for cc in range(2):
            t = f32(s2x[i, y_hi, y_lo]) if cc == 0 else f32(s2y[i, x])
            for d in range(3):
                t += f32((r2x, r2y)[cc][i, d])
            shifted = t[:, :320] + g[0:1]
            fin[i, cc, 0] = (g[1:2] * shifted).astype(jnp.bfloat16)
            fin[i, cc, 1] = (g[1:2] * t[:, 320:] + g[2:3] * shifted).astype(jnp.bfloat16)
        if i:
            send(fin.at[i, core], land.at[i, 0], fin_s.at[i, 0], fin_r.at[i, 0], at(dz=delta))
        send(fin.at[i, 1 - core], land.at[i, 1], fin_s.at[i, 1], fin_r.at[i, 1], at(dz=delta, flip=True))

    groups = ((0,), (1, 2), (3, 4), (5, 6), (7,))
    for d in range(5):
        if d:
            ring_step(1, d)
        for i in groups[d]:
            sib_wait(1, ORDER[i])
            second(i)
        if d >= 1:
            for i in groups[d - 1]:
                reduce_one(i)
        if d >= 2:
            for i in groups[d - 2]:
                reduce_two(i)
    for i in groups[3]:
        reduce_two(i)
    for i in groups[4]:
        reduce_one(i)
    for i in groups[4]:
        reduce_two(i)

    for i in range(8):
        delta = ORDER[i]
        zz = lax.rem(z - delta + 8, 8)
        for other in range(2):
            cc = 1 - core if other else core
            if i or other:
                arrived(land.at[i, other], fin_s.at[i, other], fin_r.at[i, other], at(dz=-delta, flip=bool(other)))
                src = land[i, other]
            else:
                src = fin[i, core]
            out_p[cc * 8 + zz] = src[0]
            out_t[cc * 8 + zz] = src[1]

    @pl.when(jnp.logical_not(stays))
    def _():
        for i, (src, _dst, away) in enumerate(pieces):
            copy(src, away, swap_s.at[i], swap_r.at[i], partner).wait_send()

    for c in sends:
        c.wait_send()


def shards(primal, tangent, w_in, b_in, w_out, b_out, gate_mod, gate_tan):
    x_in = jnp.concatenate([primal, tangent], 1)
    w = jnp.stack([w_in, w_out.T])
    gates = jnp.stack([b_out, gate_mod, gate_tan]).reshape(3, 16, 320).transpose(1, 0, 2)
    bf, dma = jnp.bfloat16, pltpu.SemaphoreType.DMA
    both = lambda *shape: [dma(shape), dma(shape)]
    return pl.pallas_call(
        kernel,
        out_shape=[jax.ShapeDtypeStruct((16, 16, 320), bf)] * 2,
        in_specs=[pl.BlockSpec(memory_space=pltpu.VMEM)] * 4,
        out_specs=[pl.BlockSpec(memory_space=pltpu.VMEM)] * 2,
        scratch_shapes=[
            pltpu.VMEM((2, 8, 2, 320, 864), bf),
            pltpu.VMEM((16, 256, 640), bf),
            pltpu.VMEM((2, 1, 864), jnp.float32),
            pltpu.VMEM((2, 256, 864), jnp.float32),
            pltpu.VMEM((2, 2, 128, 864), bf),
            pltpu.VMEM((8, 2, 2, 2, 4, 16, 640), bf),
            pltpu.VMEM((8, 3, 2, 2, 16, 640), bf),
            pltpu.VMEM((8, 3, 4, 16, 640), bf),
            pltpu.VMEM((8, 2, 2, 16, 640), bf),
            pltpu.VMEM((8, 4, 16, 640), bf),
            pltpu.VMEM((8, 3, 16, 640), bf),
            pltpu.VMEM((8, 3, 16, 640), bf),
            pltpu.VMEM((8, 2, 2, 16, 320), bf),
            pltpu.VMEM((8, 2, 2, 16, 320), bf),
            *both(6), dma, dma, *both(2, 2, 2, 4), *both(2, 2, 8),
            *both(2, 3), *both(2, 4, 3), *both(8, 2, 3), *both(8, 2, 3), *both(8, 2),
        ],
        compiler_params=pltpu.CompilerParams(
            collective_id=0, has_side_effects=True, vmem_limit_bytes=56 << 20
        ),
        cost_estimate=pl.CostEstimate(flops=9 * 10**9, bytes_accessed=3 * 10**6, transcendentals=221184),
        name="ffn_pair",
    )(x_in, w, b_in.reshape(1, 864), gates)


def solution(mesh):
    return jax.shard_map(
        shards,
        mesh=mesh,
        in_specs=(
            P("seq", "fsdp"),
            P("seq", "fsdp"),
            P("seq", "fsdp"),
            P("fsdp"),
            P("fsdp", "seq"),
            P(),
            P(),
            P(),
        ),
        out_specs=(P(None, "fsdp", "seq"), P(None, "fsdp", "seq")),
        check_vma=False,
    )
```

```python
import functools

import jax
import jax.numpy as jnp
from jax import lax
from jax.experimental import pallas as pl
from jax.experimental.pallas import tpu as pltpu
from jax.sharding import PartitionSpec as P

MESH = pl.DeviceIdType.MESH
ORDER = (0, 1, 7, 2, 6, 3, 5, 4)


def gelu_pair(pre):
    inner = 0.7978845608 * (pre + 0.044715 * pre * pre * pre)
    curve = jnp.tanh(inner)
    value = 0.5 * pre * (1.0 + curve)
    slope = 0.5 * (1.0 + curve) + 0.5 * pre * (1.0 - curve * curve) * 0.7978845608 * (
        1.0 + 3.0 * 0.044715 * pre * pre
    )
    return value, slope


def reach(q, way):
    return 4 if (q == 0) == (way == 1) else 3


OFF = (0, -1, 1, 2)


def kernel(
    xp_in, xt_in, w_in, w_out, b_in, b_out, gate_mod, gate_tan,
    out_p, out_t,
    wbuf, xbuf, relay_w, relay_x, bias, gates, acc, hid,
    part, r1x, r1y, s2x, s2y, r2x, r2y, fin, land,
    swap_s, swap_r, relay_s, relay_r, bias_s, bias_r, ring_s, ring_r, sib_s, sib_r,
    xs_s, xs_r, xf_s, xf_r, rs1_s, rs1_r, rs2_s, rs2_r, fin_s, fin_r,
):
    f = lax.axis_index("fsdp")
    s = lax.axis_index("seq")
    core = lax.rem(f, 2)
    x = lax.rem(f // 2, 4)
    y_lo = f // 8
    y_hi = s // 8
    z = lax.rem(s, 8)
    y = y_hi * 2 + y_lo
    sends = []

    def dev(xx, yy, zz, cc):
        return (lax.rem(yy, 2) * 8 + xx * 2 + cc, (yy // 2) * 8 + zz)

    def at(dx=0, dy=0, dz=0, flip=False):
        return dev(
            lax.rem(x + dx + 4, 4), lax.rem(y + dy + 4, 4), lax.rem(z + dz + 8, 8),
            1 - core if flip else core,
        )

    def copy(src, dst, ssem, rsem, where):
        return pltpu.make_async_remote_copy(
            src_ref=src, dst_ref=dst, send_sem=ssem, recv_sem=rsem, device_id=where, device_id_type=MESH
        )

    def send(src, dst, ssem, rsem, where):
        c = copy(src, dst, ssem, rsem, where)
        c.start()
        sends.append(c)

    def arrived(dst, ssem, rsem, where):
        copy(dst, dst, ssem, rsem, where).wait_recv()

    barrier = pltpu.get_barrier_semaphore()
    friends = [at(dz=d, flip=fl) for d in range(8) for fl in (False, True) if d or fl]
    friends += [at(dx=d) for d in (1, 2, 3)] + [at(dy=d) for d in (1, 2, 3)]
    friends += [at(dy=d, flip=True) for d in (1, 3)]
    for who in friends:
        pl.semaphore_signal(barrier, inc=1, device_id=who, device_id_type=MESH)
    pl.semaphore_wait(barrier, len(friends))

    rows = lambda q: pl.ds(q * 160, 160)
    stays = y_hi == core
    moves = jnp.logical_not(stays)
    own_k = (y_lo * 4 + x) * 2 + y_hi
    sources = [w_in.at[rows(0)], w_in.at[rows(1)], xp_in, xt_in, w_out.at[rows(0)], w_out.at[rows(1)]]
    homes = [
        wbuf.at[0, 0, core, rows(0)], wbuf.at[0, 0, core, rows(1)], xbuf.at[own_k, 0], xbuf.at[own_k, 1],
        wbuf.at[1, 0, core, rows(0)], wbuf.at[1, 0, core, rows(1)],
    ]
    relays = [relay_w.at[0], relay_w.at[0], relay_x, relay_x, relay_w.at[1], relay_w.at[1]]
    passes = [(lax.rem(y + (3 if e == 0 else 1), 4) // 2) == core for e in range(2)]
    step_of = lambda i: 1 if i % 2 == 0 else -1

    def swap_copy(i):
        return copy(sources[i], relays[i], swap_s.at[i], swap_r.at[i], at(dy=step_of(i), flip=True))

    def relay_copy(i):
        yy = lax.rem(y + step_of(i) + 4, 4)
        k = (lax.rem(yy, 2) * 4 + x) * 2 + yy // 2
        dst = xbuf.at[k, i % 2] if i in (2, 3) else homes[i]
        return copy(relays[i], dst, relay_s.at[i], relay_r.at[i], at(dy=step_of(i)))

    def swap_open(i):
        @pl.when(stays)
        def _():
            pltpu.make_async_copy(sources[i], homes[i], relay_r.at[i]).start()

        @pl.when(moves)
        def _():
            swap_copy(i).start()

    def swap_pass(i):
        for e in range(2):
            @pl.when(passes[e])
            def _():
                swap_copy(i + e).wait_recv()
                relay_copy(i + e).start()

    def own(i):
        pltpu.make_async_copy(sources[i], homes[i], relay_r.at[i]).wait()

    def w_at(h, delta, q, who=None):
        return wbuf.at[h, delta % 8, core if who is None else who, rows(q)]

    def ring_send(h, q, way, d):
        send(
            w_at(h, -way * (d - 1), q), w_at(h, -way * d, q),
            ring_s.at[h, q, (way + 1) // 2, d - 1], ring_r.at[h, q, (way + 1) // 2, d - 1], at(dz=way),
        )

    def sib_send(h, q, delta):
        send(w_at(h, delta, q), w_at(h, delta, q), sib_s.at[h, q, delta % 8], sib_r.at[h, q, delta % 8], at(flip=True))

    def sib_wait(h, delta):
        for q in range(2):
            arrived(w_at(h, delta, q, 1 - core), sib_s.at[h, q, delta % 8], sib_r.at[h, q, delta % 8], at(flip=True))

    def ring_step(h, d):
        for q in range(2):
            for way in (1, -1):
                if d > reach(q, way):
                    continue
                arrived(
                    w_at(h, -way * d, q),
                    ring_s.at[h, q, (way + 1) // 2, d - 1], ring_r.at[h, q, (way + 1) // 2, d - 1], at(dz=way),
                )
                if d < reach(q, way):
                    ring_send(h, q, way, d + 1)
                sib_send(h, q, -way * d)

    def ring_open(h, q):
        for way in (1, -1):
            ring_send(h, q, way, 1)
        sib_send(h, q, 0)

    def slot(a, o1, o2, part_of=None):
        dx, dy = (o1, o2) if a == 0 else (o2, o1)
        xx, yy = lax.rem(x + dx + 4, 4), lax.rem(y + dy + 4, 4)
        k = (lax.rem(yy, 2) * 4 + xx) * 2 + yy // 2
        return xbuf.at[k, a] if part_of is None else xbuf.at[k, a, rows(part_of)]

    def along(a, stage, d):
        return at(dx=d) if (a == 0) == (stage == 0) else at(dy=d)

    def offset(stage, r, d):
        return (d, 0) if stage == 0 else (OFF[r], d)

    def bc_open(a, stage, r=0):
        for wi, way in enumerate((1, -1)):
            src = slot(a, *offset(stage, r, 0))
            i = stage * 4 + r
            send(src, src, xs_s.at[a, i, wi], xs_r.at[a, i, wi], along(a, stage, way))

    def bc_pass(a, stage, r=0):
        for wi, way in enumerate((1, -1)):
            i = stage * 4 + r
            place = offset(stage, r, -way)
            arrived(slot(a, *place), xs_s.at[a, i, wi], xs_r.at[a, i, wi], along(a, stage, way))
            piece = slot(a, *place, wi)
            send(piece, piece, xf_s.at[a, i, wi], xf_r.at[a, i, wi], along(a, stage, way))

    def bc_end(a, stage, r=0):
        for wi, way in enumerate((1, -1)):
            i = stage * 4 + r
            arrived(slot(a, *offset(stage, r, 2), wi), xf_s.at[a, i, wi], xf_r.at[a, i, wi], along(a, stage, way))

    for i in range(4):
        swap_open(i)
    bias[core] = b_in[...].reshape(1, 864)
    send(bias.at[core], bias.at[core], bias_s, bias_r, at(flip=True))
    swap_pass(0)
    for q in range(2):
        own(q)
        ring_open(0, q)
    swap_pass(2)
    for a in range(2):
        own(2 + a)
        bc_open(a, 0)
        bc_open(a, 1, 0)
    acc[...] = jnp.zeros_like(acc)
    for n, table in enumerate((b_out, gate_mod, gate_tan)):
        for i in range(16):
            first_row, lane = i * 320 // 128, i * 320 % 128
            flat = jnp.concatenate([table[first_row + j : first_row + j + 1, :] for j in range(3)], axis=1)
            gates[i, n : n + 1] = flat[:, lane : lane + 320]
    ring_step(0, 1)
    for a in range(2):
        bc_pass(a, 0)
        for r in (1, 2):
            bc_open(a, 1, r)
    for a in range(2):
        bc_pass(a, 1, 0)
    for a in range(2):
        bc_end(a, 0)
        bc_open(a, 1, 3)
    for i in (4, 5):
        swap_open(i)
    ring_step(0, 2)
    for r in (1, 2):
        for a in range(2):
            bc_pass(a, 1, r)
    swap_pass(4)
    for a in range(2):
        bc_pass(a, 1, 3)
    ring_step(0, 3)
    for q in range(2):
        own(4 + q)
        ring_open(1, q)
    for r in range(4):
        for a in range(2):
            bc_end(a, 1, r)
    ring_step(0, 4)
    for delta in ORDER:
        sib_wait(0, delta)
    arrived(bias.at[1 - core], bias_s, bias_r, at(flip=True))

    def first(i, carry):
        delta, h = i // 2, lax.rem(i, 2)
        k = h * 8 + lax.rem(z + delta, 8)
        w = wbuf[0, delta, h]
        for a in range(2):
            acc[a] += lax.dot_general(xbuf[k, a], w, (((0,), (0,)), ((), ())), preferred_element_type=jnp.float32)
        return carry

    lax.fori_loop(0, 16, first, 0)

    def activate(i, carry):
        r = pl.ds(pl.multiple_of(i * 32, 32), 32)
        into = pl.ds(pl.multiple_of(lax.rem(i, 4) * 32, 32), 32)
        value, slope = gelu_pair(acc[0, r, :] + bias[y_hi])
        hid[i // 4, 0, into, :] = value.astype(jnp.bfloat16)
        hid[i // 4, 1, into, :] = (slope * acc[1, r, :]).astype(jnp.bfloat16)
        return carry

    lax.fori_loop(0, 8, activate, 0)

    def second(i):
        delta = ORDER[i]

        def body(j, carry):
            h, yl = j // 2, lax.rem(j, 2)
            both = lax.dot_general(
                hid[yl].reshape(256, 864), wbuf[1, delta, h], (((1,), (1,)), ((), ())),
                preferred_element_type=jnp.float32,
            )
            packed = jnp.concatenate([both[:128], both[128:]], axis=1).astype(jnp.bfloat16)
            for b in range(8):
                part[i, b % 2, h, yl, b // 2] = packed[b * 16 : (b + 1) * 16]
            return carry

        lax.fori_loop(0, 4, body, 0)
        for d in (1, 2, 3):
            xx = lax.rem(x + d, 4)
            send(part.at[i, 0, :, :, xx], r1x.at[i, d - 1], rs1_s.at[i, 0, d - 1], rs1_r.at[i, 0, d - 1], at(dx=d))
            yy = lax.rem(y + d, 4)
            send(
                part.at[i, 1, yy // 2, lax.rem(yy, 2)], r1y.at[i, d - 1],
                rs1_s.at[i, 1, d - 1], rs1_r.at[i, 1, d - 1], at(dy=d),
            )

    f32 = lambda v: v.astype(jnp.float32)

    def reduce_one(i):
        for d in (1, 2, 3):
            arrived(r1x.at[i, d - 1], rs1_s.at[i, 0, d - 1], rs1_r.at[i, 0, d - 1], at(dx=-d))
        for h in range(2):
            for yl in range(2):
                t = f32(part[i, 0, h, yl, x])
                for d in range(3):
                    t += f32(r1x[i, d, h, yl])
                s2x[i, h, yl] = t.astype(jnp.bfloat16)
        for d in (1, 2, 3):
            yy = lax.rem(y + d, 4)
            send(
                s2x.at[i, yy // 2, lax.rem(yy, 2)], r2x.at[i, d - 1],
                rs2_s.at[i, 0, d - 1], rs2_r.at[i, 0, d - 1], at(dy=d),
            )
        for d in (1, 2, 3):
            arrived(r1y.at[i, d - 1], rs1_s.at[i, 1, d - 1], rs1_r.at[i, 1, d - 1], at(dy=-d))
        for b in range(4):
            t = f32(part[i, 1, y_hi, y_lo, b])
            for d in range(3):
                t += f32(r1y[i, d, b])
            s2y[i, b] = t.astype(jnp.bfloat16)
        for d in (1, 2, 3):
            send(s2y.at[i, lax.rem(x + d, 4)], r2y.at[i, d - 1], rs2_s.at[i, 1, d - 1], rs2_r.at[i, 1, d - 1], at(dx=d))

    def reduce_two(i):
        delta = ORDER[i]
        g = gates[y_hi * 8 + lax.rem(z + delta, 8)]
        for d in (1, 2, 3):
            arrived(r2x.at[i, d - 1], rs2_s.at[i, 0, d - 1], rs2_r.at[i, 0, d - 1], at(dy=-d))
            arrived(r2y.at[i, d - 1], rs2_s.at[i, 1, d - 1], rs2_r.at[i, 1, d - 1], at(dx=-d))
        for cc in range(2):
            t = f32(s2x[i, y_hi, y_lo]) if cc == 0 else f32(s2y[i, x])
            for d in range(3):
                t += f32((r2x, r2y)[cc][i, d])
            shifted = t[:, :320] + g[0:1]
            fin[i, cc, 0] = (g[1:2] * shifted).astype(jnp.bfloat16)
            fin[i, cc, 1] = (g[1:2] * t[:, 320:] + g[2:3] * shifted).astype(jnp.bfloat16)
        if i:
            send(fin.at[i, core], land.at[i, 0], fin_s.at[i, 0], fin_r.at[i, 0], at(dz=delta))
        send(fin.at[i, 1 - core], land.at[i, 1], fin_s.at[i, 1], fin_r.at[i, 1], at(dz=delta, flip=True))

    groups = ((0,), (1, 2), (3, 4), (5, 6), (7,))
    for d in range(5):
        if d:
            ring_step(1, d)
        for i in groups[d]:
            sib_wait(1, ORDER[i])
            second(i)
        if d >= 1:
            for i in groups[d - 1]:
                reduce_one(i)
        if d >= 2:
            for i in groups[d - 2]:
                reduce_two(i)
    for i in groups[3]:
        reduce_two(i)
    for i in groups[4]:
        reduce_one(i)
    for i in groups[4]:
        reduce_two(i)

    for i in range(8):
        delta = ORDER[i]
        zz = lax.rem(z - delta + 8, 8)
        for other in range(2):
            cc = 1 - core if other else core
            if i or other:
                arrived(land.at[i, other], fin_s.at[i, other], fin_r.at[i, other], at(dz=-delta, flip=bool(other)))
                src = land[i, other]
            else:
                src = fin[i, core]
            out_p[cc * 8 + zz] = src[0]
            out_t[cc * 8 + zz] = src[1]

    @pl.when(moves)
    def _():
        for i in range(6):
            swap_copy(i).wait_send()

    for e in range(2):
        @pl.when(passes[e])
        def _():
            for i in (0, 2, 4):
                relay_copy(i + e).wait_send()

    for c in sends:
        c.wait_send()


def shards(primal, tangent, w_in, b_in, w_out, b_out, gate_mod, gate_tan):
    tables = [t.reshape(40, 128) for t in (b_out, gate_mod, gate_tan)]
    bf, dma = jnp.bfloat16, pltpu.SemaphoreType.DMA
    both = lambda *shape: [dma(shape), dma(shape)]
    return pl.pallas_call(
        kernel,
        out_shape=[jax.ShapeDtypeStruct((16, 16, 320), bf)] * 2,
        in_specs=[pl.BlockSpec(memory_space=pltpu.VMEM)] * 8,
        out_specs=[pl.BlockSpec(memory_space=pltpu.VMEM)] * 2,
        scratch_shapes=[
            pltpu.VMEM((2, 8, 2, 320, 864), bf),
            pltpu.VMEM((16, 2, 320, 256), bf),
            pltpu.VMEM((2, 160, 864), bf),
            pltpu.VMEM((320, 256), bf),
            pltpu.VMEM((2, 1, 864), jnp.float32),
            pltpu.VMEM((16, 3, 320), jnp.float32),
            pltpu.VMEM((2, 256, 864), jnp.float32),
            pltpu.VMEM((2, 2, 128, 864), bf),
            pltpu.VMEM((8, 2, 2, 2, 4, 16, 640), bf),
            pltpu.VMEM((8, 3, 2, 2, 16, 640), bf),
            pltpu.VMEM((8, 3, 4, 16, 640), bf),
            pltpu.VMEM((8, 2, 2, 16, 640), bf),
            pltpu.VMEM((8, 4, 16, 640), bf),
            pltpu.VMEM((8, 3, 16, 640), bf),
            pltpu.VMEM((8, 3, 16, 640), bf),
            pltpu.VMEM((8, 2, 2, 16, 320), bf),
            pltpu.VMEM((8, 2, 2, 16, 320), bf),
            *both(6), *both(6), dma, dma, *both(2, 2, 2, 4), *both(2, 2, 8),
            *both(2, 8, 2), *both(2, 8, 2), *both(8, 2, 3), *both(8, 2, 3), *both(8, 2),
        ],
        compiler_params=pltpu.CompilerParams(
            collective_id=0, has_side_effects=True, vmem_limit_bytes=56 << 20
        ),
        cost_estimate=pl.CostEstimate(flops=9 * 10**9, bytes_accessed=3 * 10**6, transcendentals=221184),
        name="ffn_pair",
    )(primal.T, tangent.T, w_in, w_out.T, b_in, *tables)


def solution(mesh):
    return jax.shard_map(
        shards,
        mesh=mesh,
        in_specs=(
            P("seq", "fsdp"),
            P("seq", "fsdp"),
            P("seq", "fsdp"),
            P("fsdp"),
            P("fsdp", "seq"),
            P(),
            P(),
            P(),
        ),
        out_specs=(P(None, "fsdp", "seq"), P(None, "fsdp", "seq")),
        check_vma=False,
    )
```

```python
import functools

import jax
import jax.numpy as jnp
from jax import lax
from jax.experimental import pallas as pl
from jax.experimental.pallas import tpu as pltpu
from jax.sharding import PartitionSpec as P

MESH = pl.DeviceIdType.MESH
ORDER = (0, 1, 7, 2, 6, 3, 5, 4)


def gelu_pair(pre):
    inner = 0.7978845608 * (pre + 0.044715 * pre * pre * pre)
    curve = jnp.tanh(inner)
    value = 0.5 * pre * (1.0 + curve)
    slope = 0.5 * (1.0 + curve) + 0.5 * pre * (1.0 - curve * curve) * 0.7978845608 * (
        1.0 + 3.0 * 0.044715 * pre * pre
    )
    return value, slope


def reach(q, way):
    return 4 if (q == 0) == (way == 1) else 3


OFF = (0, -1, 1, 2)


def kernel(
    xp_in, xt_in, w_in, w_out, b_in, b_out, gate_mod, gate_tan,
    out_p, out_t,
    wbuf, xbuf, relay_w, relay_x, bias, gates, acc, hid,
    part, r0, r1, s2, r2, fin, land,
    swap_s, swap_r, relay_s, relay_r, bias_s, bias_r, ring_s, ring_r, sib_s, sib_r,
    xs_s, xs_r, xf_s, xf_r, rs0_s, rs0_r, rs1_s, rs1_r, rs2_s, rs2_r, fin_s, fin_r,
):
    f = lax.axis_index("fsdp")
    s = lax.axis_index("seq")
    core = lax.rem(f, 2)
    x = lax.rem(f // 2, 4)
    y_lo = f // 8
    y_hi = s // 8
    z = lax.rem(s, 8)
    y = y_hi * 2 + y_lo
    sends = []

    def dev(xx, yy, zz, cc):
        return (lax.rem(yy, 2) * 8 + xx * 2 + cc, (yy // 2) * 8 + zz)

    def at(dx=0, dy=0, dz=0, flip=False):
        return dev(
            lax.rem(x + dx + 4, 4), lax.rem(y + dy + 4, 4), lax.rem(z + dz + 8, 8),
            1 - core if flip else core,
        )

    def copy(src, dst, ssem, rsem, where):
        return pltpu.make_async_remote_copy(
            src_ref=src, dst_ref=dst, send_sem=ssem, recv_sem=rsem, device_id=where, device_id_type=MESH
        )

    def send(src, dst, ssem, rsem, where, mode="start, note"):
        if "start" in mode:
            copy(src, dst, ssem, rsem, where).start()
        if "note" in mode:
            sends.append((src, dst, ssem, rsem, where))

    def arrived(dst, ssem, rsem, where):
        copy(dst, dst, ssem, rsem, where).wait_recv()

    barrier = pltpu.get_barrier_semaphore()
    friends = [at(dz=d, flip=fl) for d in range(8) for fl in (False, True) if d or fl]
    friends += [at(dx=d) for d in (1, 2, 3)] + [at(dy=d) for d in (1, 2, 3)]
    friends += [at(dy=d, flip=True) for d in (1, 3)]
    for who in friends:
        pl.semaphore_signal(barrier, inc=1, device_id=who, device_id_type=MESH)
    pl.semaphore_wait(barrier, len(friends))

    rows = lambda q: pl.ds(q * 160, 160)
    stays = y_hi == core
    moves = jnp.logical_not(stays)
    own_k = (y_lo * 4 + x) * 2 + y_hi
    sources = [w_in.at[rows(0)], w_in.at[rows(1)], xp_in, xt_in, w_out.at[rows(0)], w_out.at[rows(1)]]
    homes = [
        wbuf.at[0, 0, core, rows(0)], wbuf.at[0, 0, core, rows(1)], xbuf.at[own_k, 0], xbuf.at[own_k, 1],
        wbuf.at[1, 0, core, rows(0)], wbuf.at[1, 0, core, rows(1)],
    ]
    relays = [relay_w.at[0], relay_w.at[0], relay_x, relay_x, relay_w.at[1], relay_w.at[1]]
    passes = [(lax.rem(y + (3 if e == 0 else 1), 4) // 2) == core for e in range(2)]
    step_of = lambda i: 1 if i % 2 == 0 else -1

    def swap_copy(i):
        return copy(sources[i], relays[i], swap_s.at[i], swap_r.at[i], at(dy=step_of(i), flip=True))

    def relay_copy(i):
        yy = lax.rem(y + step_of(i) + 4, 4)
        k = (lax.rem(yy, 2) * 4 + x) * 2 + yy // 2
        dst = xbuf.at[k, i % 2] if i in (2, 3) else homes[i]
        return copy(relays[i], dst, relay_s.at[i], relay_r.at[i], at(dy=step_of(i)))

    def swap_open(i):
        @pl.when(stays)
        def _():
            pltpu.make_async_copy(sources[i], homes[i], relay_r.at[i]).start()

        @pl.when(moves)
        def _():
            swap_copy(i).start()

    def swap_pass(i):
        for e in range(2):
            @pl.when(passes[e])
            def _():
                swap_copy(i + e).wait_recv()
                relay_copy(i + e).start()

    def own(i):
        pltpu.make_async_copy(sources[i], homes[i], relay_r.at[i]).wait()

    def w_at(h, delta, q, who=None):
        return wbuf.at[h, delta % 8, core if who is None else who, rows(q)]

    def ring_send(h, q, way, d, mode="start, note"):
        send(
            w_at(h, -way * (d - 1), q), w_at(h, -way * d, q),
            ring_s.at[h, q, (way + 1) // 2, d - 1], ring_r.at[h, q, (way + 1) // 2, d - 1], at(dz=way), mode,
        )

    def sib_send(h, q, delta, mode="start, note"):
        send(w_at(h, delta, q), w_at(h, delta, q), sib_s.at[h, q, delta % 8], sib_r.at[h, q, delta % 8], at(flip=True), mode)

    def sib_wait(h, delta):
        for q in range(2):
            arrived(w_at(h, delta, q, 1 - core), sib_s.at[h, q, delta % 8], sib_r.at[h, q, delta % 8], at(flip=True))

    def ring_step(h, d):
        for q in range(2):
            for way in (1, -1):
                if d > reach(q, way):
                    continue
                arrived(
                    w_at(h, -way * d, q),
                    ring_s.at[h, q, (way + 1) // 2, d - 1], ring_r.at[h, q, (way + 1) // 2, d - 1], at(dz=way),
                )
                if d < reach(q, way):
                    ring_send(h, q, way, d + 1)
                sib_send(h, q, -way * d)

    def ring_open(h, q, mode="start, note"):
        for way in (1, -1):
            ring_send(h, q, way, 1, mode)
        sib_send(h, q, 0, mode)

    def slot(a, o1, o2, part_of=None):
        dx, dy = (o1, o2) if a == 0 else (o2, o1)
        xx, yy = lax.rem(x + dx + 4, 4), lax.rem(y + dy + 4, 4)
        k = (lax.rem(yy, 2) * 4 + xx) * 2 + yy // 2
        return xbuf.at[k, a] if part_of is None else xbuf.at[k, a, rows(part_of)]

    def along(a, stage, d):
        return at(dx=d) if (a == 0) == (stage == 0) else at(dy=d)

    def offset(stage, r, d):
        return (d, 0) if stage == 0 else (OFF[r], d)

    def bc_open(a, stage, r=0, mode="start, note"):
        for wi, way in enumerate((1, -1)):
            src = slot(a, *offset(stage, r, 0))
            i = stage * 4 + r
            send(src, src, xs_s.at[a, i, wi], xs_r.at[a, i, wi], along(a, stage, way), mode)

    def bc_pass(a, stage, r=0):
        for wi, way in enumerate((1, -1)):
            i = stage * 4 + r
            place = offset(stage, r, -way)
            arrived(slot(a, *place), xs_s.at[a, i, wi], xs_r.at[a, i, wi], along(a, stage, way))
            piece = slot(a, *place, wi)
            send(piece, piece, xf_s.at[a, i, wi], xf_r.at[a, i, wi], along(a, stage, way))

    def bc_end(a, stage, r=0):
        for wi, way in enumerate((1, -1)):
            i = stage * 4 + r
            arrived(slot(a, *offset(stage, r, 2), wi), xf_s.at[a, i, wi], xf_r.at[a, i, wi], along(a, stage, way))

    for i in range(4):
        swap_open(i)
    bias[core] = b_in[...].reshape(1, 864)
    send(bias.at[core], bias.at[core], bias_s, bias_r, at(flip=True))

    def open_w(mode):
        for q in range(2):
            if mode == "start":
                own(q)
            ring_open(0, q, mode)

    def open_x(mode):
        for a in range(2):
            if mode == "start":
                own(2 + a)
            bc_open(a, 0, 0, mode)
            bc_open(a, 1, 0, mode)

    @pl.when(stays)
    def _():
        open_w("start")
        open_x("start")

    swap_pass(0)

    @pl.when(moves)
    def _():
        open_w("start")

    swap_pass(2)

    @pl.when(moves)
    def _():
        open_x("start")

    open_w("note")
    open_x("note")
    acc[...] = jnp.zeros_like(acc)
    for n, table in enumerate((b_out, gate_mod, gate_tan)):
        for i in range(16):
            first_row, lane = i * 320 // 128, i * 320 % 128
            flat = jnp.concatenate([table[first_row + j : first_row + j + 1, :] for j in range(3)], axis=1)
            gates[i, n : n + 1] = flat[:, lane : lane + 320]
    ring_step(0, 1)
    for a in range(2):
        bc_pass(a, 0)
        for r in (1, 2):
            bc_open(a, 1, r)
    for a in range(2):
        bc_pass(a, 1, 0)
    for a in range(2):
        bc_end(a, 0)
        bc_open(a, 1, 3)
    for i in (4, 5):
        swap_open(i)
    ring_step(0, 2)
    for r in (1, 2):
        for a in range(2):
            bc_pass(a, 1, r)
    swap_pass(4)
    for a in range(2):
        bc_pass(a, 1, 3)
    ring_step(0, 3)
    for q in range(2):
        own(4 + q)
        ring_open(1, q)
    for r in range(4):
        for a in range(2):
            bc_end(a, 1, r)

    def first(i, carry):
        delta, h = lax.rem(i // 2 + 6, 8), lax.rem(i, 2)
        k = h * 8 + lax.rem(z + delta, 8)
        w = wbuf[0, delta, h]
        for a in range(2):
            acc[a] += lax.dot_general(xbuf[k, a], w, (((0,), (0,)), ((), ())), preferred_element_type=jnp.float32)
        return carry

    for delta in ORDER[:5]:
        sib_wait(0, delta)
    lax.fori_loop(0, 10, first, 0)
    ring_step(0, 4)
    for delta in ORDER[5:]:
        sib_wait(0, delta)
    lax.fori_loop(10, 16, first, 0)
    arrived(bias.at[1 - core], bias_s, bias_r, at(flip=True))

    def activate(i, carry):
        r = pl.ds(pl.multiple_of(i * 32, 32), 32)
        into = pl.ds(pl.multiple_of(lax.rem(i, 4) * 32, 32), 32)
        value, slope = gelu_pair(acc[0, r, :] + bias[y_hi])
        hid[i // 4, 0, into, :] = value.astype(jnp.bfloat16)
        hid[i // 4, 1, into, :] = (slope * acc[1, r, :]).astype(jnp.bfloat16)
        return carry

    lax.fori_loop(0, 8, activate, 0)

    def second(i):
        delta = ORDER[i]

        def body(j, carry):
            h, yl = j // 2, lax.rem(j, 2)
            both = lax.dot_general(
                hid[yl].reshape(256, 864), wbuf[1, delta, h], (((1,), (1,)), ((), ())),
                preferred_element_type=jnp.float32,
            )
            packed = jnp.concatenate([both[:128], both[128:]], axis=1).astype(jnp.bfloat16)
            for b in range(4):
                part[i, 0, b, j] = packed[b * 32 : b * 32 + 16]
                part[i, 1, j, b] = packed[b * 32 + 16 : b * 32 + 32]
            return carry

        lax.fori_loop(0, 4, body, 0)
        for a in range(2):
            for wi, way in enumerate((1, -1)):
                send(
                    part.at[i, a, there(a, 2), pl.ds(2 * wi, 2)], r0.at[i, a, wi],
                    rs0_s.at[i, a, wi], rs0_r.at[i, a, wi], along(a, 0, way),
                )

    f32 = lambda v: v.astype(jnp.float32)

    def there(a, d):
        return lax.rem((x if a == 0 else y) + d + 4, 4)

    def reduce_zero(i):
        for a in range(2):
            for wi, way in enumerate((1, -1)):
                arrived(r0.at[i, a, wi], rs0_s.at[i, a, wi], rs0_r.at[i, a, wi], along(a, 0, way))
                j = there(a, way)
                for b in range(2):
                    t = f32(part[i, a, j, 2 * wi + b]) + f32(r0[i, a, wi, b])
                    part[i, a, j, 2 * wi + b] = t.astype(jnp.bfloat16)
                send(part.at[i, a, j], r1.at[i, a, wi], rs1_s.at[i, a, wi], rs1_r.at[i, a, wi], along(a, 0, way))

    def reduce_one(i):
        for a in range(2):
            for wi, way in enumerate((1, -1)):
                arrived(r1.at[i, a, wi], rs1_s.at[i, a, wi], rs1_r.at[i, a, wi], along(a, 0, way))
            for b in range(4):
                t = f32(part[i, a, there(a, 0), b]) + f32(r1[i, a, 0, b]) + f32(r1[i, a, 1, b])
                s2[i, a, b] = t.astype(jnp.bfloat16)
            for d in (1, 2, 3):
                send(
                    s2.at[i, a, there(1 - a, d)], r2.at[i, a, d - 1],
                    rs2_s.at[i, a, d - 1], rs2_r.at[i, a, d - 1], along(a, 1, d),
                )

    def reduce_two(i):
        delta = ORDER[i]
        g = gates[y_hi * 8 + lax.rem(z + delta, 8)]
        for d in (1, 2, 3):
            for a in range(2):
                arrived(r2.at[i, a, d - 1], rs2_s.at[i, a, d - 1], rs2_r.at[i, a, d - 1], along(a, 1, d))
        for cc in range(2):
            t = f32(s2[i, cc, there(1 - cc, 0)])
            for d in range(3):
                t += f32(r2[i, cc, d])
            shifted = t[:, :320] + g[0:1]
            fin[i, cc, 0] = (g[1:2] * shifted).astype(jnp.bfloat16)
            fin[i, cc, 1] = (g[1:2] * t[:, 320:] + g[2:3] * shifted).astype(jnp.bfloat16)
        if i:
            send(fin.at[i, core], land.at[i, 0], fin_s.at[i, 0], fin_r.at[i, 0], at(dz=delta))
        send(fin.at[i, 1 - core], land.at[i, 1], fin_s.at[i, 1], fin_r.at[i, 1], at(dz=delta, flip=True))

    def each(what, *items):
        for i in items:
            what(i)

    def blocks(d, *items):
        if d:
            ring_step(1, d)
        for i in items:
            sib_wait(1, ORDER[i])
            second(i)

    blocks(0, 0)
    blocks(1, 1, 2)
    each(reduce_zero, 0)
    each(reduce_one, 0)
    each(reduce_zero, 1, 2)
    each(reduce_one, 1, 2)
    blocks(2, 3, 4)
    each(reduce_two, 0, 1, 2)
    each(reduce_zero, 3, 4)
    each(reduce_one, 3, 4)
    blocks(3, 5, 6)
    each(reduce_two, 3, 4)
    each(reduce_zero, 5, 6)
    blocks(4, 7)
    each(reduce_one, 5, 6)
    each(reduce_zero, 7)
    each(reduce_two, 5, 6)
    each(reduce_one, 7)
    each(reduce_two, 7)

    for i in range(8):
        delta = ORDER[i]
        zz = lax.rem(z - delta + 8, 8)
        for other in range(2):
            cc = 1 - core if other else core
            if i or other:
                arrived(land.at[i, other], fin_s.at[i, other], fin_r.at[i, other], at(dz=-delta, flip=bool(other)))
                src = land[i, other]
            else:
                src = fin[i, core]
            out_p[cc * 8 + zz] = src[0]
            out_t[cc * 8 + zz] = src[1]

    @pl.when(moves)
    def _():
        for i in range(6):
            swap_copy(i).wait_send()

    for e in range(2):
        @pl.when(passes[e])
        def _():
            for i in (0, 2, 4):
                relay_copy(i + e).wait_send()

    for c in sends:
        copy(*c).wait_send()


def shards(primal, tangent, w_in, b_in, w_out, b_out, gate_mod, gate_tan):
    tables = [t.reshape(40, 128) for t in (b_out, gate_mod, gate_tan)]
    bf, dma = jnp.bfloat16, pltpu.SemaphoreType.DMA
    both = lambda *shape: [dma(shape), dma(shape)]
    return pl.pallas_call(
        kernel,
        out_shape=[jax.ShapeDtypeStruct((16, 16, 320), bf)] * 2,
        in_specs=[pl.BlockSpec(memory_space=pltpu.VMEM)] * 8,
        out_specs=[pl.BlockSpec(memory_space=pltpu.VMEM)] * 2,
        scratch_shapes=[
            pltpu.VMEM((2, 8, 2, 320, 864), bf),
            pltpu.VMEM((16, 2, 320, 256), bf),
            pltpu.VMEM((2, 160, 864), bf),
            pltpu.VMEM((320, 256), bf),
            pltpu.VMEM((2, 1, 864), jnp.float32),
            pltpu.VMEM((16, 3, 320), jnp.float32),
            pltpu.VMEM((2, 256, 864), jnp.float32),
            pltpu.VMEM((2, 2, 128, 864), bf),
            pltpu.VMEM((8, 2, 4, 4, 16, 640), bf),
            pltpu.VMEM((8, 2, 2, 2, 16, 640), bf),
            pltpu.VMEM((8, 2, 2, 4, 16, 640), bf),
            pltpu.VMEM((8, 2, 4, 16, 640), bf),
            pltpu.VMEM((8, 2, 3, 16, 640), bf),
            pltpu.VMEM((8, 2, 2, 16, 320), bf),
            pltpu.VMEM((8, 2, 2, 16, 320), bf),
            *both(6), *both(6), dma, dma, *both(2, 2, 2, 4), *both(2, 2, 8),
            *both(2, 8, 2), *both(2, 8, 2), *both(8, 2, 2), *both(8, 2, 2), *both(8, 2, 3), *both(8, 2),
        ],
        compiler_params=pltpu.CompilerParams(
            collective_id=0, has_side_effects=True, vmem_limit_bytes=56 << 20
        ),
        cost_estimate=pl.CostEstimate(flops=9 * 10**9, bytes_accessed=3 * 10**6, transcendentals=221184),
        name="ffn_pair",
    )(primal.T, tangent.T, w_in, w_out.T, b_in, *tables)


def solution(mesh):
    return jax.shard_map(
        shards,
        mesh=mesh,
        in_specs=(
            P("seq", "fsdp"),
            P("seq", "fsdp"),
            P("seq", "fsdp"),
            P("fsdp"),
            P("fsdp", "seq"),
            P(),
            P(),
            P(),
        ),
        out_specs=(P(None, "fsdp", "seq"), P(None, "fsdp", "seq")),
        check_vma=False,
    )
```

```python
import functools

import jax
import jax.numpy as jnp
from jax import lax
from jax.experimental import pallas as pl
from jax.experimental.pallas import tpu as pltpu
from jax.sharding import PartitionSpec as P

MESH = pl.DeviceIdType.MESH
ORDER = (0, 1, 7, 2, 6, 3, 5, 4)


def gelu_pair(pre):
    inner = 0.7978845608 * (pre + 0.044715 * pre * pre * pre)
    curve = jnp.tanh(inner)
    value = 0.5 * pre * (1.0 + curve)
    slope = 0.5 * (1.0 + curve) + 0.5 * pre * (1.0 - curve * curve) * 0.7978845608 * (
        1.0 + 3.0 * 0.044715 * pre * pre
    )
    return value, slope


def reach(q, way):
    return 4 if (q == 0) == (way == 1) else 3


OFF = (0, -1, 1, 2)


def kernel(
    xp_in, xt_in, w_in, w_out, b_in, b_out, gate_mod, gate_tan,
    out_p, out_t,
    wbuf, xbuf, relay_w, relay_x, bias, gates, acc, hid,
    part, r0, r1, s2, r2, fin, land,
    swap_s, swap_r, relay_s, relay_r, bias_s, bias_r, ring_s, ring_r, sib_s, sib_r,
    xs_s, xs_r, xf_s, xf_r, rs0_s, rs0_r, rs1_s, rs1_r, rs2_s, rs2_r, fin_s, fin_r,
):
    f = lax.axis_index("fsdp")
    s = lax.axis_index("seq")
    core = lax.rem(f, 2)
    x = lax.rem(f // 2, 4)
    y_lo = f // 8
    y_hi = s // 8
    z = lax.rem(s, 8)
    y = y_hi * 2 + y_lo
    sends = []

    def dev(xx, yy, zz, cc):
        return (lax.rem(yy, 2) * 8 + xx * 2 + cc, (yy // 2) * 8 + zz)

    def at(dx=0, dy=0, dz=0, flip=False):
        return dev(
            lax.rem(x + dx + 4, 4), lax.rem(y + dy + 4, 4), lax.rem(z + dz + 8, 8),
            1 - core if flip else core,
        )

    def copy(src, dst, ssem, rsem, where):
        return pltpu.make_async_remote_copy(
            src_ref=src, dst_ref=dst, send_sem=ssem, recv_sem=rsem, device_id=where, device_id_type=MESH
        )

    mode = ["start, note"]

    def send(src, dst, ssem, rsem, where):
        if "start" in mode[0]:
            copy(src, dst, ssem, rsem, where).start()
        if "note" in mode[0]:
            sends.append((src, dst, ssem, rsem, where))

    def arrived(dst, ssem, rsem, where):
        if "start" in mode[0]:
            copy(dst, dst, ssem, rsem, where).wait_recv()

    barrier = pltpu.get_barrier_semaphore()
    friends = [at(dz=d, flip=fl) for d in range(8) for fl in (False, True) if d or fl]
    friends += [at(dx=d) for d in (1, 2, 3)] + [at(dy=d) for d in (1, 2, 3)]
    friends += [at(dy=d, flip=True) for d in (1, 3)]
    for who in friends:
        pl.semaphore_signal(barrier, inc=1, device_id=who, device_id_type=MESH)
    pl.semaphore_wait(barrier, len(friends))

    rows = lambda q: pl.ds(q * 160, 160)
    stays = y_hi == core
    moves = jnp.logical_not(stays)
    sources = [w_in.at[rows(0)], w_in.at[rows(1)], xp_in, xt_in, w_out.at[rows(0)], w_out.at[rows(1)]]
    homes = [
        wbuf.at[0, 0, core, rows(0)], wbuf.at[0, 0, core, rows(1)], xbuf.at[x * 2 + y_hi, 0, y_lo], xbuf.at[x * 2 + y_hi, 1, y_lo],
        wbuf.at[1, 0, core, rows(0)], wbuf.at[1, 0, core, rows(1)],
    ]
    relays = [relay_w.at[0], relay_w.at[0], relay_x, relay_x, relay_w.at[1], relay_w.at[1]]
    passes = [(lax.rem(y + (3 if e == 0 else 1), 4) // 2) == core for e in range(2)]
    step_of = lambda i: 1 if i % 2 == 0 else -1

    def swap_copy(i):
        return copy(sources[i], relays[i], swap_s.at[i], swap_r.at[i], at(dy=step_of(i), flip=True))

    def relay_copy(i):
        yy = lax.rem(y + step_of(i) + 4, 4)
        dst = xbuf.at[x * 2 + yy // 2, i % 2, lax.rem(yy, 2)] if i in (2, 3) else homes[i]
        return copy(relays[i], dst, relay_s.at[i], relay_r.at[i], at(dy=step_of(i)))

    def swap_open(i):
        @pl.when(stays)
        def _():
            pltpu.make_async_copy(sources[i], homes[i], relay_r.at[i]).start()

        @pl.when(moves)
        def _():
            swap_copy(i).start()

    def swap_pass(i):
        for e in range(2):
            @pl.when(passes[e])
            def _():
                swap_copy(i + e).wait_recv()
                relay_copy(i + e).start()

    def own(i):
        pltpu.make_async_copy(sources[i], homes[i], relay_r.at[i]).wait()

    def w_at(h, delta, q, who=None):
        return wbuf.at[h, delta % 8, core if who is None else who, rows(q)]

    def ring_send(h, q, way, d):
        send(
            w_at(h, -way * (d - 1), q), w_at(h, -way * d, q),
            ring_s.at[h, q, (way + 1) // 2, d - 1], ring_r.at[h, q, (way + 1) // 2, d - 1], at(dz=way),
        )

    def sib_send(h, q, delta):
        send(w_at(h, delta, q), w_at(h, delta, q), sib_s.at[h, q, delta % 8], sib_r.at[h, q, delta % 8], at(flip=True))

    def sib_wait(h, delta):
        for q in range(2):
            arrived(w_at(h, delta, q, 1 - core), sib_s.at[h, q, delta % 8], sib_r.at[h, q, delta % 8], at(flip=True))

    def ring_step(h, d):
        for q in range(2):
            for way in (1, -1):
                if d > reach(q, way):
                    continue
                arrived(
                    w_at(h, -way * d, q),
                    ring_s.at[h, q, (way + 1) // 2, d - 1], ring_r.at[h, q, (way + 1) // 2, d - 1], at(dz=way),
                )
                if d < reach(q, way):
                    ring_send(h, q, way, d + 1)
                sib_send(h, q, -way * d)

    def ring_open(h, q):
        for way in (1, -1):
            ring_send(h, q, way, 1)
        sib_send(h, q, 0)

    def slot(a, o1, o2, part_of=None):
        dx, dy = (o1, o2) if a == 0 else (o2, o1)
        xx, yy = lax.rem(x + dx + 4, 4), lax.rem(y + dy + 4, 4)
        whole = (xx * 2 + yy // 2, a, lax.rem(yy, 2))
        return xbuf.at[whole] if part_of is None else xbuf.at[(*whole, rows(part_of))]

    def along(a, stage, d):
        return at(dx=d) if (a == 0) == (stage == 0) else at(dy=d)

    def offset(stage, r, d):
        return (d, 0) if stage == 0 else (OFF[r], d)

    def bc_open(a, stage, r=0):
        for wi, way in enumerate((1, -1)):
            src = slot(a, *offset(stage, r, 0))
            i = stage * 4 + r
            send(src, src, xs_s.at[a, i, wi], xs_r.at[a, i, wi], along(a, stage, way))

    def bc_pass(a, stage, r=0):
        for wi, way in enumerate((1, -1)):
            i = stage * 4 + r
            place = offset(stage, r, -way)
            arrived(slot(a, *place), xs_s.at[a, i, wi], xs_r.at[a, i, wi], along(a, stage, way))
            piece = slot(a, *place, wi)
            send(piece, piece, xf_s.at[a, i, wi], xf_r.at[a, i, wi], along(a, stage, way))

    def bc_end(a, stage, r=0):
        for wi, way in enumerate((1, -1)):
            i = stage * 4 + r
            arrived(slot(a, *offset(stage, r, 2), wi), xf_s.at[a, i, wi], xf_r.at[a, i, wi], along(a, stage, way))

    def branch(when, what):
        mode[0] = "start"
        pl.when(when)(what)
        mode[0] = "start, note"

    def note(what):
        mode[0] = "note"
        what()
        mode[0] = "start, note"

    def open_w():
        for q in range(2):
            if "start" in mode[0]:
                own(q)
            ring_open(0, q)

    def open_x():
        for a in range(2):
            bc_open(a, 0, 0)
            bc_open(a, 1, 0)

    def x_head():
        for a in range(2):
            bc_pass(a, 0)
            for r in (1, 2):
                bc_open(a, 1, r)
        for a in range(2):
            bc_pass(a, 1, 0)
        for a in range(2):
            bc_end(a, 0)
            bc_open(a, 1, 3)

    def x_tail():
        for r in (1, 2):
            for a in range(2):
                bc_pass(a, 1, r)

    for i in (2, 3, 0, 1):
        swap_open(i)
    bias[core] = b_in[...].reshape(1, 864)
    send(bias.at[core], bias.at[core], bias_s, bias_r, at(flip=True))

    branch(stays, open_w)
    swap_pass(2)
    swap_pass(0)
    for a in range(2):
        own(2 + a)
    open_x()
    branch(moves, open_w)
    note(open_w)
    acc[...] = jnp.zeros_like(acc)
    for n, table in enumerate((b_out, gate_mod, gate_tan)):
        for i in range(16):
            first_row, lane = i * 320 // 128, i * 320 % 128
            flat = jnp.concatenate([table[first_row + j : first_row + j + 1, :] for j in range(3)], axis=1)
            gates[i, n : n + 1] = flat[:, lane : lane + 320]
    ring_step(0, 1)
    x_head()
    ring_step(0, 2)
    x_tail()
    for i in (4, 5):
        swap_open(i)
    for a in range(2):
        bc_pass(a, 1, 3)
    swap_pass(4)
    ring_step(0, 3)
    for q in range(2):
        own(4 + q)
        ring_open(1, q)
    for r in range(4):
        for a in range(2):
            bc_end(a, 1, r)

    def first(i, carry):
        delta = lax.rem(i + 6, 8)
        w = wbuf[0, delta].reshape(640, 864)
        for a in range(2):
            xk = xbuf[lax.rem(z + delta, 8), a].reshape(640, 256)
            acc[a] += lax.dot_general(xk, w, (((0,), (0,)), ((), ())), preferred_element_type=jnp.float32)
        return carry

    for delta in ORDER[:5]:
        sib_wait(0, delta)
    lax.fori_loop(0, 5, first, 0)
    ring_step(0, 4)
    for delta in ORDER[5:]:
        sib_wait(0, delta)
    lax.fori_loop(5, 8, first, 0)
    arrived(bias.at[1 - core], bias_s, bias_r, at(flip=True))

    def activate(i, carry):
        r = pl.ds(pl.multiple_of(i * 32, 32), 32)
        into = pl.ds(pl.multiple_of(lax.rem(i, 4) * 32, 32), 32)
        value, slope = gelu_pair(acc[0, r, :] + bias[y_hi])
        hid[i // 4, 0, into, :] = value.astype(jnp.bfloat16)
        hid[i // 4, 1, into, :] = (slope * acc[1, r, :]).astype(jnp.bfloat16)
        return carry

    lax.fori_loop(0, 8, activate, 0)

    def second(i):
        delta = ORDER[i]

        def body(h, carry):
            both = lax.dot_general(
                hid[...].reshape(512, 864), wbuf[1, delta, h], (((1,), (1,)), ((), ())),
                preferred_element_type=jnp.float32,
            )
            for yl in range(2):
                packed = jnp.concatenate(
                    [both[yl * 256 : yl * 256 + 128], both[yl * 256 + 128 : yl * 256 + 256]], axis=1
                ).astype(jnp.bfloat16)
                for b in range(4):
                    part[i, 0, b, h * 2 + yl] = packed[b * 32 : b * 32 + 16]
                    part[i, 1, h * 2 + yl, b] = packed[b * 32 + 16 : b * 32 + 32]
            return carry

        lax.fori_loop(0, 2, body, 0)
        for a in range(2):
            for wi, way in enumerate((1, -1)):
                send(
                    part.at[i, a, there(a, 2), pl.ds(2 * wi, 2)], r0.at[i, a, wi],
                    rs0_s.at[i, a, wi], rs0_r.at[i, a, wi], along(a, 0, way),
                )

    f32 = lambda v: v.astype(jnp.float32)

    def there(a, d):
        return lax.rem((x if a == 0 else y) + d + 4, 4)

    def reduce_zero(i):
        for a in range(2):
            for wi, way in enumerate((1, -1)):
                arrived(r0.at[i, a, wi], rs0_s.at[i, a, wi], rs0_r.at[i, a, wi], along(a, 0, way))
                j = there(a, way)
                for b in range(2):
                    t = f32(part[i, a, j, 2 * wi + b]) + f32(r0[i, a, wi, b])
                    part[i, a, j, 2 * wi + b] = t.astype(jnp.bfloat16)
                send(part.at[i, a, j], r1.at[i, a, wi], rs1_s.at[i, a, wi], rs1_r.at[i, a, wi], along(a, 0, way))

    def reduce_one(i):
        for a in range(2):
            for wi, way in enumerate((1, -1)):
                arrived(r1.at[i, a, wi], rs1_s.at[i, a, wi], rs1_r.at[i, a, wi], along(a, 0, way))
            for b in range(4):
                t = f32(part[i, a, there(a, 0), b]) + f32(r1[i, a, 0, b]) + f32(r1[i, a, 1, b])
                s2[i, a, b] = t.astype(jnp.bfloat16)
            for d in (1, 2, 3):
                send(
                    s2.at[i, a, there(1 - a, d)], r2.at[i, a, d - 1],
                    rs2_s.at[i, a, d - 1], rs2_r.at[i, a, d - 1], along(a, 1, d),
                )

    def reduce_two(i):
        delta = ORDER[i]
        g = gates[y_hi * 8 + lax.rem(z + delta, 8)]
        for d in (1, 2, 3):
            for a in range(2):
                arrived(r2.at[i, a, d - 1], rs2_s.at[i, a, d - 1], rs2_r.at[i, a, d - 1], along(a, 1, d))
        for cc in range(2):
            t = f32(s2[i, cc, there(1 - cc, 0)])
            for d in range(3):
                t += f32(r2[i, cc, d])
            shifted = t[:, :320] + g[0:1]
            fin[i, cc, 0] = (g[1:2] * shifted).astype(jnp.bfloat16)
            fin[i, cc, 1] = (g[1:2] * t[:, 320:] + g[2:3] * shifted).astype(jnp.bfloat16)
        if i:
            send(fin.at[i, core], land.at[i, 0], fin_s.at[i, 0], fin_r.at[i, 0], at(dz=delta))
        send(fin.at[i, 1 - core], land.at[i, 1], fin_s.at[i, 1], fin_r.at[i, 1], at(dz=delta, flip=True))

    def each(what, *items):
        for i in items:
            what(i)

    def blocks(d, *items):
        if d:
            ring_step(1, d)
        for i in items:
            sib_wait(1, ORDER[i])
            second(i)

    blocks(0, 0)
    blocks(1, 1, 2)
    each(reduce_zero, 0, 1, 2)
    each(reduce_one, 0)
    blocks(2, 3, 4)
    each(reduce_one, 1, 2)
    each(reduce_zero, 3, 4)
    each(reduce_two, 0)
    blocks(3, 5, 6)
    each(reduce_one, 3, 4)
    each(reduce_zero, 5, 6)
    each(reduce_two, 1, 2)
    blocks(4, 7)
    each(reduce_one, 5, 6)
    each(reduce_zero, 7)
    each(reduce_two, 3, 4, 5, 6)
    each(reduce_one, 7)
    each(reduce_two, 7)

    for i in range(8):
        delta = ORDER[i]
        zz = lax.rem(z - delta + 8, 8)
        for other in range(2):
            cc = 1 - core if other else core
            if i or other:
                arrived(land.at[i, other], fin_s.at[i, other], fin_r.at[i, other], at(dz=-delta, flip=bool(other)))
                src = land[i, other]
            else:
                src = fin[i, core]
            out_p[cc * 8 + zz] = src[0]
            out_t[cc * 8 + zz] = src[1]

    @pl.when(moves)
    def _():
        for i in range(6):
            swap_copy(i).wait_send()

    for e in range(2):
        @pl.when(passes[e])
        def _():
            for i in (0, 2, 4):
                relay_copy(i + e).wait_send()

    for c in sends:
        copy(*c).wait_send()


def shards(primal, tangent, w_in, b_in, w_out, b_out, gate_mod, gate_tan):
    tables = [t.reshape(40, 128) for t in (b_out, gate_mod, gate_tan)]
    bf, dma = jnp.bfloat16, pltpu.SemaphoreType.DMA
    both = lambda *shape: [dma(shape), dma(shape)]
    return pl.pallas_call(
        kernel,
        out_shape=[jax.ShapeDtypeStruct((16, 16, 320), bf)] * 2,
        in_specs=[pl.BlockSpec(memory_space=pltpu.VMEM)] * 8,
        out_specs=[pl.BlockSpec(memory_space=pltpu.VMEM)] * 2,
        scratch_shapes=[
            pltpu.VMEM((2, 8, 2, 320, 864), bf),
            pltpu.VMEM((8, 2, 2, 320, 256), bf),
            pltpu.VMEM((2, 160, 864), bf),
            pltpu.VMEM((320, 256), bf),
            pltpu.VMEM((2, 1, 864), jnp.float32),
            pltpu.VMEM((16, 3, 320), jnp.float32),
            pltpu.VMEM((2, 256, 864), jnp.float32),
            pltpu.VMEM((2, 2, 128, 864), bf),
            pltpu.VMEM((8, 2, 4, 4, 16, 640), bf),
            pltpu.VMEM((8, 2, 2, 2, 16, 640), bf),
            pltpu.VMEM((8, 2, 2, 4, 16, 640), bf),
            pltpu.VMEM((8, 2, 4, 16, 640), bf),
            pltpu.VMEM((8, 2, 3, 16, 640), bf),
            pltpu.VMEM((8, 2, 2, 16, 320), bf),
            pltpu.VMEM((8, 2, 2, 16, 320), bf),
            *both(6), *both(6), dma, dma, *both(2, 2, 2, 4), *both(2, 2, 8),
            *both(2, 8, 2), *both(2, 8, 2), *both(8, 2, 2), *both(8, 2, 2), *both(8, 2, 3), *both(8, 2),
        ],
        compiler_params=pltpu.CompilerParams(
            collective_id=0, has_side_effects=True, vmem_limit_bytes=56 << 20
        ),
        cost_estimate=pl.CostEstimate(flops=9 * 10**9, bytes_accessed=3 * 10**6, transcendentals=221184),
        name="ffn_pair",
    )(primal.T, tangent.T, w_in, w_out.T, b_in, *tables)


def solution(mesh):
    return jax.shard_map(
        shards,
        mesh=mesh,
        in_specs=(
            P("seq", "fsdp"),
            P("seq", "fsdp"),
            P("seq", "fsdp"),
            P("fsdp"),
            P("fsdp", "seq"),
            P(),
            P(),
            P(),
        ),
        out_specs=(P(None, "fsdp", "seq"), P(None, "fsdp", "seq")),
        check_vma=False,
    )
```

```python
import functools

import jax
import jax.numpy as jnp
from jax import lax
from jax.experimental import pallas as pl
from jax.experimental.pallas import tpu as pltpu
from jax.sharding import PartitionSpec as P

MESH = pl.DeviceIdType.MESH
ORDER = (0, 1, 7, 2, 6, 3, 5, 4)


def gelu_pair(pre):
    inner = 0.7978845608 * (pre + 0.044715 * pre * pre * pre)
    curve = jnp.tanh(inner)
    value = 0.5 * pre * (1.0 + curve)
    slope = 0.5 * (1.0 + curve) + 0.5 * pre * (1.0 - curve * curve) * 0.7978845608 * (
        1.0 + 3.0 * 0.044715 * pre * pre
    )
    return value, slope


def reach(q, way):
    return 4 if (q == 0) == (way == 1) else 3


OFF = (0, -1, 1, 2)


def kernel(
    xp_in, xt_in, w_in, w_out, b_in, b_out, gate_mod, gate_tan,
    out_p, out_t,
    wbuf, xbuf, relay_w, relay_x, bias, gates, acc, hid,
    part, r0, r1, s2, r2, fin, land,
    swap_s, swap_r, relay_s, relay_r, bias_s, bias_r, ring_s, ring_r, sib_s, sib_r,
    xs_s, xs_r, xf_s, xf_r, rs0_s, rs0_r, rs1_s, rs1_r, rs2_s, rs2_r, fin_s, fin_r,
):
    f = lax.axis_index("fsdp")
    s = lax.axis_index("seq")
    core = lax.rem(f, 2)
    x = lax.rem(f // 2, 4)
    y_lo = f // 8
    y_hi = s // 8
    z = lax.rem(s, 8)
    y = y_hi * 2 + y_lo
    sends = []

    def dev(xx, yy, zz, cc):
        return (lax.rem(yy, 2) * 8 + xx * 2 + cc, (yy // 2) * 8 + zz)

    def at(dx=0, dy=0, dz=0, flip=False):
        return dev(
            lax.rem(x + dx + 4, 4), lax.rem(y + dy + 4, 4), lax.rem(z + dz + 8, 8),
            1 - core if flip else core,
        )

    def copy(src, dst, ssem, rsem, where):
        return pltpu.make_async_remote_copy(
            src_ref=src, dst_ref=dst, send_sem=ssem, recv_sem=rsem, device_id=where, device_id_type=MESH
        )

    mode = ["start, note"]

    def send(src, dst, ssem, rsem, where):
        if "start" in mode[0]:
            copy(src, dst, ssem, rsem, where).start()
        if "note" in mode[0]:
            sends.append((src, dst, ssem, rsem, where))

    def arrived(dst, ssem, rsem, where):
        if "start" in mode[0]:
            copy(dst, dst, ssem, rsem, where).wait_recv()

    barrier = pltpu.get_barrier_semaphore()
    friends = [at(dz=d) for d in (1, 7)] + [at(flip=True)]
    friends += [at(dx=d) for d in (1, 3)] + [at(dy=d) for d in (1, 3)]
    friends += [at(dy=d, flip=True) for d in (1, 3)]
    for who in friends:
        pl.semaphore_signal(barrier, inc=1, device_id=who, device_id_type=MESH)
    pl.semaphore_wait(barrier, len(friends))

    rows = lambda q: pl.ds(q * 160, 160)
    stays = y_hi == core
    moves = jnp.logical_not(stays)
    eighty = lambda n: pl.ds(n * 80, 80)
    sources = [w_in.at[eighty(0)], w_in.at[eighty(1)], xp_in, xt_in, w_out.at[rows(0)], w_out.at[rows(1)]]
    sources += [w_in.at[eighty(2)], w_in.at[eighty(3)]]
    homes = [
        wbuf.at[0, 0, core, eighty(0)], wbuf.at[0, 0, core, eighty(1)], xbuf.at[x * 2 + y_hi, 0, y_lo], xbuf.at[x * 2 + y_hi, 1, y_lo],
        wbuf.at[1, 0, core, rows(0)], wbuf.at[1, 0, core, rows(1)],
        wbuf.at[0, 0, core, eighty(2)], wbuf.at[0, 0, core, eighty(3)],
    ]
    relays = [relay_w.at[0, eighty(0)]] * 2 + [relay_x] * 2 + [relay_w.at[1]] * 2 + [relay_w.at[0, eighty(1)]] * 2
    passes = [(lax.rem(y + (3 if e == 0 else 1), 4) // 2) == core for e in range(2)]
    step_of = lambda i: 1 if i % 2 == 0 else -1

    def swap_copy(i):
        return copy(sources[i], relays[i], swap_s.at[i], swap_r.at[i], at(dy=step_of(i), flip=True))

    def relay_copy(i):
        yy = lax.rem(y + step_of(i) + 4, 4)
        dst = xbuf.at[x * 2 + yy // 2, i % 2, lax.rem(yy, 2)] if i in (2, 3) else homes[i]
        return copy(relays[i], dst, relay_s.at[i], relay_r.at[i], at(dy=step_of(i)))

    def swap_open(i):
        @pl.when(stays)
        def _():
            pltpu.make_async_copy(sources[i], homes[i], relay_r.at[i]).start()

        @pl.when(moves)
        def _():
            swap_copy(i).start()

    def swap_pass(i):
        for e in range(2):
            @pl.when(passes[e])
            def _():
                swap_copy(i + e).wait_recv()
                relay_copy(i + e).start()

    def own(i):
        pltpu.make_async_copy(sources[i], homes[i], relay_r.at[i]).wait()

    def w_at(h, delta, q, who=None):
        return wbuf.at[h, delta % 8, core if who is None else who, rows(q)]

    def ring_send(h, q, way, d):
        send(
            w_at(h, -way * (d - 1), q), w_at(h, -way * d, q),
            ring_s.at[h, q, (way + 1) // 2, d - 1], ring_r.at[h, q, (way + 1) // 2, d - 1], at(dz=way),
        )

    def sib_send(h, q, delta):
        send(w_at(h, delta, q), w_at(h, delta, q), sib_s.at[h, q, delta % 8], sib_r.at[h, q, delta % 8], at(flip=True))

    def sib_wait(h, delta):
        for q in range(2):
            arrived(w_at(h, delta, q, 1 - core), sib_s.at[h, q, delta % 8], sib_r.at[h, q, delta % 8], at(flip=True))

    def ring_step(h, d):
        for q in range(2):
            for way in (1, -1):
                if d > reach(q, way):
                    continue
                arrived(
                    w_at(h, -way * d, q),
                    ring_s.at[h, q, (way + 1) // 2, d - 1], ring_r.at[h, q, (way + 1) // 2, d - 1], at(dz=way),
                )
                if d < reach(q, way):
                    ring_send(h, q, way, d + 1)
                sib_send(h, q, -way * d)

    def ring_open(h, q):
        for way in (1, -1):
            ring_send(h, q, way, 1)
        sib_send(h, q, 0)

    def slot(a, o1, o2, part_of=None):
        dx, dy = (o1, o2) if a == 0 else (o2, o1)
        xx, yy = lax.rem(x + dx + 4, 4), lax.rem(y + dy + 4, 4)
        whole = (xx * 2 + yy // 2, a, lax.rem(yy, 2))
        return xbuf.at[whole] if part_of is None else xbuf.at[(*whole, rows(part_of))]

    def along(a, stage, d):
        return at(dx=d) if (a == 0) == (stage == 0) else at(dy=d)

    def offset(stage, r, d):
        return (d, 0) if stage == 0 else (OFF[r], d)

    def bc_open(a, stage, r=0):
        for wi, way in enumerate((1, -1)):
            src = slot(a, *offset(stage, r, 0))
            i = stage * 4 + r
            send(src, src, xs_s.at[a, i, wi], xs_r.at[a, i, wi], along(a, stage, way))

    def bc_pass(a, stage, r=0):
        for wi, way in enumerate((1, -1)):
            i = stage * 4 + r
            place = offset(stage, r, -way)
            arrived(slot(a, *place), xs_s.at[a, i, wi], xs_r.at[a, i, wi], along(a, stage, way))
            piece = slot(a, *place, wi)
            send(piece, piece, xf_s.at[a, i, wi], xf_r.at[a, i, wi], along(a, stage, way))

    def bc_end(a, stage, r=0):
        for wi, way in enumerate((1, -1)):
            i = stage * 4 + r
            arrived(slot(a, *offset(stage, r, 2), wi), xf_s.at[a, i, wi], xf_r.at[a, i, wi], along(a, stage, way))

    def branch(when, what):
        mode[0] = "start"
        pl.when(when)(what)
        mode[0] = "start, note"

    def note(what):
        mode[0] = "note"
        what()
        mode[0] = "start, note"

    def open_w():
        for q in range(2):
            if "start" in mode[0]:
                own(6 * q)
                own(6 * q + 1)
            ring_open(0, q)

    def open_x():
        for a in range(2):
            bc_open(a, 0, 0)
            bc_open(a, 1, 0)

    def x_head():
        for a in range(2):
            bc_pass(a, 0)
            for r in (1, 2):
                bc_open(a, 1, r)
        for a in range(2):
            bc_pass(a, 1, 0)
        for a in range(2):
            bc_end(a, 0)
            bc_open(a, 1, 3)

    def x_tail():
        for r in (1, 2):
            for a in range(2):
                bc_pass(a, 1, r)

    for i in (2, 3, 0, 1, 6, 7):
        swap_open(i)
    bias[core] = b_in[...].reshape(1, 864)
    send(bias.at[core], bias.at[core], bias_s, bias_r, at(flip=True))

    branch(stays, open_w)
    swap_pass(2)
    swap_pass(0)
    swap_pass(6)
    for a in range(2):
        own(2 + a)
    open_x()
    branch(moves, open_w)
    note(open_w)
    acc[...] = jnp.zeros_like(acc)
    for n, table in enumerate((b_out, gate_mod, gate_tan)):
        for i in range(16):
            first_row, lane = i * 320 // 128, i * 320 % 128
            flat = jnp.concatenate([table[first_row + j : first_row + j + 1, :] for j in range(3)], axis=1)
            gates[i, n : n + 1] = flat[:, lane : lane + 320]
    ring_step(0, 1)
    x_head()
    ring_step(0, 2)
    x_tail()
    for i in (4, 5):
        swap_open(i)
    for a in range(2):
        bc_pass(a, 1, 3)
    swap_pass(4)
    ring_step(0, 3)
    for q in range(2):
        own(4 + q)
        ring_open(1, q)
    for r in range(4):
        for a in range(2):
            bc_end(a, 1, r)

    def first(i, carry):
        delta = lax.rem(i + 6, 8)
        w = wbuf[0, delta].reshape(640, 864)
        for a in range(2):
            xk = xbuf[lax.rem(z + delta, 8), a].reshape(640, 256)
            acc[a] += lax.dot_general(xk, w, (((0,), (0,)), ((), ())), preferred_element_type=jnp.float32)
        return carry

    for delta in ORDER[:5]:
        sib_wait(0, delta)
    lax.fori_loop(0, 5, first, 0)
    ring_step(0, 4)
    for delta in ORDER[5:]:
        sib_wait(0, delta)
    lax.fori_loop(5, 8, first, 0)
    ring_step(1, 1)
    arrived(bias.at[1 - core], bias_s, bias_r, at(flip=True))

    def activate(i, carry):
        r = pl.ds(pl.multiple_of(i * 32, 32), 32)
        into = pl.ds(pl.multiple_of(lax.rem(i, 4) * 32, 32), 32)
        value, slope = gelu_pair(acc[0, r, :] + bias[y_hi])
        hid[i // 4, 0, into, :] = value.astype(jnp.bfloat16)
        hid[i // 4, 1, into, :] = (slope * acc[1, r, :]).astype(jnp.bfloat16)
        return carry

    lax.fori_loop(0, 8, activate, 0)

    def second(i):
        delta = ORDER[i]

        def body(h, carry):
            both = lax.dot_general(
                hid[...].reshape(512, 864), wbuf[1, delta, h], (((1,), (1,)), ((), ())),
                preferred_element_type=jnp.float32,
            )
            for yl in range(2):
                packed = jnp.concatenate(
                    [both[yl * 256 : yl * 256 + 128], both[yl * 256 + 128 : yl * 256 + 256]], axis=1
                ).astype(jnp.bfloat16)
                for b in range(4):
                    part[i, 0, b, h * 2 + yl] = packed[b * 32 : b * 32 + 16]
                    part[i, 1, h * 2 + yl, b] = packed[b * 32 + 16 : b * 32 + 32]
            return carry

        lax.fori_loop(0, 2, body, 0)
        for a in range(2):
            for wi, way in enumerate((1, -1)):
                send(
                    part.at[i, a, there(a, 2), pl.ds(2 * wi, 2)], r0.at[i, a, wi],
                    rs0_s.at[i, a, wi], rs0_r.at[i, a, wi], along(a, 0, way),
                )

    f32 = lambda v: v.astype(jnp.float32)

    def there(a, d):
        return lax.rem((x if a == 0 else y) + d + 4, 4)

    def reduce_zero(i):
        for a in range(2):
            for wi, way in enumerate((1, -1)):
                arrived(r0.at[i, a, wi], rs0_s.at[i, a, wi], rs0_r.at[i, a, wi], along(a, 0, way))
                j = there(a, way)
                for b in range(2):
                    t = f32(part[i, a, j, 2 * wi + b]) + f32(r0[i, a, wi, b])
                    part[i, a, j, 2 * wi + b] = t.astype(jnp.bfloat16)
                send(part.at[i, a, j], r1.at[i, a, wi], rs1_s.at[i, a, wi], rs1_r.at[i, a, wi], along(a, 0, way))

    def reduce_one(i):
        for a in range(2):
            for wi, way in enumerate((1, -1)):
                arrived(r1.at[i, a, wi], rs1_s.at[i, a, wi], rs1_r.at[i, a, wi], along(a, 0, way))
            for b in range(4):
                t = f32(part[i, a, there(a, 0), b]) + f32(r1[i, a, 0, b]) + f32(r1[i, a, 1, b])
                s2[i, a, b] = t.astype(jnp.bfloat16)
            for d in (1, 2, 3):
                send(
                    s2.at[i, a, there(1 - a, d)], r2.at[i, a, d - 1],
                    rs2_s.at[i, a, d - 1], rs2_r.at[i, a, d - 1], along(a, 1, d),
                )

    def reduce_two(i):
        delta = ORDER[i]
        g = gates[y_hi * 8 + lax.rem(z + delta, 8)]
        for d in (1, 2, 3):
            for a in range(2):
                arrived(r2.at[i, a, d - 1], rs2_s.at[i, a, d - 1], rs2_r.at[i, a, d - 1], along(a, 1, d))
        for cc in range(2):
            t = f32(s2[i, cc, there(1 - cc, 0)])
            for d in range(3):
                t += f32(r2[i, cc, d])
            shifted = t[:, :320] + g[0:1]
            fin[i, cc, 0] = (g[1:2] * shifted).astype(jnp.bfloat16)
            fin[i, cc, 1] = (g[1:2] * t[:, 320:] + g[2:3] * shifted).astype(jnp.bfloat16)
        if i:
            send(fin.at[i, core], land.at[i, 0], fin_s.at[i, 0], fin_r.at[i, 0], at(dz=delta))
        send(fin.at[i, 1 - core], land.at[i, 1], fin_s.at[i, 1], fin_r.at[i, 1], at(dz=delta, flip=True))

    def each(what, *items):
        for i in items:
            what(i)

    def block(i):
        sib_wait(1, ORDER[i])
        second(i)

    block(0)
    block(1)
    reduce_zero(0)
    block(2)
    reduce_one(0)
    each(reduce_zero, 1, 2)
    ring_step(1, 2)
    block(3)
    reduce_one(1)
    block(4)
    reduce_one(2)
    reduce_two(0)
    each(reduce_zero, 3, 4)
    ring_step(1, 3)
    block(5)
    reduce_one(3)
    block(6)
    reduce_one(4)
    each(reduce_two, 1, 2)
    each(reduce_zero, 5, 6)
    ring_step(1, 4)
    block(7)
    each(reduce_one, 5, 6)
    reduce_zero(7)
    each(reduce_two, 3, 4, 5, 6)
    reduce_one(7)
    reduce_two(7)

    for i in range(8):
        delta = ORDER[i]
        zz = lax.rem(z - delta + 8, 8)
        for other in range(2):
            cc = 1 - core if other else core
            if i or other:
                arrived(land.at[i, other], fin_s.at[i, other], fin_r.at[i, other], at(dz=-delta, flip=bool(other)))
                src = land[i, other]
            else:
                src = fin[i, core]
            out_p[cc * 8 + zz] = src[0]
            out_t[cc * 8 + zz] = src[1]

    @pl.when(moves)
    def _():
        for i in range(8):
            swap_copy(i).wait_send()

    for e in range(2):
        @pl.when(passes[e])
        def _():
            for i in (0, 2, 4, 6):
                relay_copy(i + e).wait_send()

    for c in sends:
        copy(*c).wait_send()


def shards(primal, tangent, w_in, b_in, w_out, b_out, gate_mod, gate_tan):
    tables = [t.reshape(40, 128) for t in (b_out, gate_mod, gate_tan)]
    bf, dma = jnp.bfloat16, pltpu.SemaphoreType.DMA
    both = lambda *shape: [dma(shape), dma(shape)]
    return pl.pallas_call(
        kernel,
        out_shape=[jax.ShapeDtypeStruct((16, 16, 320), bf)] * 2,
        in_specs=[pl.BlockSpec(memory_space=pltpu.VMEM)] * 8,
        out_specs=[pl.BlockSpec(memory_space=pltpu.VMEM)] * 2,
        scratch_shapes=[
            pltpu.VMEM((2, 8, 2, 320, 864), bf),
            pltpu.VMEM((8, 2, 2, 320, 256), bf),
            pltpu.VMEM((2, 160, 864), bf),
            pltpu.VMEM((320, 256), bf),
            pltpu.VMEM((2, 1, 864), jnp.float32),
            pltpu.VMEM((16, 3, 320), jnp.float32),
            pltpu.VMEM((2, 256, 864), jnp.float32),
            pltpu.VMEM((2, 2, 128, 864), bf),
            pltpu.VMEM((8, 2, 4, 4, 16, 640), bf),
            pltpu.VMEM((8, 2, 2, 2, 16, 640), bf),
            pltpu.VMEM((8, 2, 2, 4, 16, 640), bf),
            pltpu.VMEM((8, 2, 4, 16, 640), bf),
            pltpu.VMEM((8, 2, 3, 16, 640), bf),
            pltpu.VMEM((8, 2, 2, 16, 320), bf),
            pltpu.VMEM((8, 2, 2, 16, 320), bf),
            *both(8), *both(8), dma, dma, *both(2, 2, 2, 4), *both(2, 2, 8),
            *both(2, 8, 2), *both(2, 8, 2), *both(8, 2, 2), *both(8, 2, 2), *both(8, 2, 3), *both(8, 2),
        ],
        compiler_params=pltpu.CompilerParams(
            collective_id=0, has_side_effects=True, vmem_limit_bytes=56 << 20
        ),
        cost_estimate=pl.CostEstimate(flops=9 * 10**9, bytes_accessed=3 * 10**6, transcendentals=221184),
        name="ffn_pair",
    )(primal.T, tangent.T, w_in, w_out.T, b_in, *tables)


def solution(mesh):
    return jax.shard_map(
        shards,
        mesh=mesh,
        in_specs=(
            P("seq", "fsdp"),
            P("seq", "fsdp"),
            P("seq", "fsdp"),
            P("fsdp"),
            P("fsdp", "seq"),
            P(),
            P(),
            P(),
        ),
        out_specs=(P(None, "fsdp", "seq"), P(None, "fsdp", "seq")),
        check_vma=False,
    )
```

```python
import functools

import jax
import jax.numpy as jnp
from jax import lax
from jax.experimental import pallas as pl
from jax.experimental.pallas import tpu as pltpu
from jax.sharding import PartitionSpec as P

MESH = pl.DeviceIdType.MESH
ORDER = (0, 1, 7, 2, 6, 3, 5, 4)


def gelu_pair(pre):
    inner = 0.7978845608 * (pre + 0.044715 * pre * pre * pre)
    curve = jnp.tanh(inner)
    value = 0.5 * pre * (1.0 + curve)
    slope = 0.5 * (1.0 + curve) + 0.5 * pre * (1.0 - curve * curve) * 0.7978845608 * (
        1.0 + 3.0 * 0.044715 * pre * pre
    )
    return value, slope


def reach(q, way):
    return 4 if (q == 0) == (way == 1) else 3


OFF = (0, -1, 1, 2)


def kernel(
    xp_in, xt_in, w_in, w_out, b_in, b_out, gate_mod, gate_tan,
    out,
    wbuf, xbuf, relay_w, relay_x, bias, gates, acc, hid,
    part, r0, r1, s2, r2, fin, land,
    swap_s, swap_r, relay_s, relay_r, bias_s, bias_r, ring_s, ring_r, sib_s, sib_r,
    xs_s, xs_r, xf_s, xf_r, rs0_s, rs0_r, rs1_s, rs1_r, rs2_s, rs2_r, fin_s, fin_r,
):
    f = lax.axis_index("fsdp")
    s = lax.axis_index("seq")
    core = lax.rem(f, 2)
    x = lax.rem(f // 2, 4)
    y_lo = f // 8
    y_hi = s // 8
    z = lax.rem(s, 8)
    y = y_hi * 2 + y_lo
    sends = []

    def dev(xx, yy, zz, cc):
        return (lax.rem(yy, 2) * 8 + xx * 2 + cc, (yy // 2) * 8 + zz)

    def at(dx=0, dy=0, dz=0, flip=False):
        return dev(
            lax.rem(x + dx + 4, 4), lax.rem(y + dy + 4, 4), lax.rem(z + dz + 8, 8),
            1 - core if flip else core,
        )

    def copy(src, dst, ssem, rsem, where):
        return pltpu.make_async_remote_copy(
            src_ref=src, dst_ref=dst, send_sem=ssem, recv_sem=rsem, device_id=where, device_id_type=MESH
        )

    mode = ["start, note"]

    def send(src, dst, ssem, rsem, where):
        if "start" in mode[0]:
            copy(src, dst, ssem, rsem, where).start()
        if "note" in mode[0]:
            sends.append((src, dst, ssem, rsem, where))

    def arrived(dst, ssem, rsem, where):
        if "start" in mode[0]:
            copy(dst, dst, ssem, rsem, where).wait_recv()

    barrier = pltpu.get_barrier_semaphore()
    friends = [at(dz=d) for d in (1, 7)] + [at(flip=True)]
    friends += [at(dx=d) for d in (1, 3)] + [at(dy=d) for d in (1, 3)]
    friends += [at(dy=d, flip=True) for d in (1, 3)]
    for who in friends:
        pl.semaphore_signal(barrier, inc=1, device_id=who, device_id_type=MESH)
    pl.semaphore_wait(barrier, len(friends))

    rows = lambda q: pl.ds(q * 160, 160)
    stays = y_hi == core
    moves = jnp.logical_not(stays)
    eighty = lambda n: pl.ds(n * 80, 80)
    sources = [w_in.at[eighty(0)], w_in.at[eighty(1)], xp_in, xt_in, w_out.at[rows(0)], w_out.at[rows(1)]]
    sources += [w_in.at[eighty(2)], w_in.at[eighty(3)]]
    homes = [
        wbuf.at[0, 0, core, eighty(0)], wbuf.at[0, 0, core, eighty(1)], xbuf.at[x * 2 + y_hi, 0, y_lo], xbuf.at[x * 2 + y_hi, 1, y_lo],
        wbuf.at[1, 0, core, rows(0)], wbuf.at[1, 0, core, rows(1)],
        wbuf.at[0, 0, core, eighty(2)], wbuf.at[0, 0, core, eighty(3)],
    ]
    relays = [relay_w.at[0, eighty(0)]] * 2 + [relay_x] * 2 + [relay_w.at[1]] * 2 + [relay_w.at[0, eighty(1)]] * 2
    passes = [(lax.rem(y + (3 if e == 0 else 1), 4) // 2) == core for e in range(2)]
    step_of = lambda i: 1 if i % 2 == 0 else -1

    def swap_copy(i):
        return copy(sources[i], relays[i], swap_s.at[i], swap_r.at[i], at(dy=step_of(i), flip=True))

    def relay_copy(i):
        yy = lax.rem(y + step_of(i) + 4, 4)
        dst = xbuf.at[x * 2 + yy // 2, i % 2, lax.rem(yy, 2)] if i in (2, 3) else homes[i]
        return copy(relays[i], dst, relay_s.at[i], relay_r.at[i], at(dy=step_of(i)))

    def swap_open(i):
        @pl.when(stays)
        def _():
            pltpu.make_async_copy(sources[i], homes[i], relay_r.at[i]).start()

        @pl.when(moves)
        def _():
            swap_copy(i).start()

    def swap_pass(i):
        for e in range(2):
            @pl.when(passes[e])
            def _():
                swap_copy(i + e).wait_recv()
                relay_copy(i + e).start()

    def own(i):
        pltpu.make_async_copy(sources[i], homes[i], relay_r.at[i]).wait()

    def w_at(h, delta, q, who=None):
        return wbuf.at[h, delta % 8, core if who is None else who, rows(q)]

    def ring_send(h, q, way, d):
        send(
            w_at(h, -way * (d - 1), q), w_at(h, -way * d, q),
            ring_s.at[h, q, (way + 1) // 2, d - 1], ring_r.at[h, q, (way + 1) // 2, d - 1], at(dz=way),
        )

    def sib_send(h, q, delta):
        send(w_at(h, delta, q), w_at(h, delta, q), sib_s.at[h, q, delta % 8], sib_r.at[h, q, delta % 8], at(flip=True))

    def sib_wait(h, delta):
        for q in range(2):
            arrived(w_at(h, delta, q, 1 - core), sib_s.at[h, q, delta % 8], sib_r.at[h, q, delta % 8], at(flip=True))

    def ring_step(h, d):
        for q in range(2):
            for way in (1, -1):
                if d > reach(q, way):
                    continue
                arrived(
                    w_at(h, -way * d, q),
                    ring_s.at[h, q, (way + 1) // 2, d - 1], ring_r.at[h, q, (way + 1) // 2, d - 1], at(dz=way),
                )
                if d < reach(q, way):
                    ring_send(h, q, way, d + 1)
                sib_send(h, q, -way * d)

    def ring_open(h, q):
        for way in (1, -1):
            ring_send(h, q, way, 1)
        sib_send(h, q, 0)

    def slot(a, o1, o2, part_of=None):
        dx, dy = (o1, o2) if a == 0 else (o2, o1)
        xx, yy = lax.rem(x + dx + 4, 4), lax.rem(y + dy + 4, 4)
        whole = (xx * 2 + yy // 2, a, lax.rem(yy, 2))
        return xbuf.at[whole] if part_of is None else xbuf.at[(*whole, rows(part_of))]

    def along(a, stage, d):
        return at(dx=d) if (a == 0) == (stage == 0) else at(dy=d)

    def offset(stage, r, d):
        return (d, 0) if stage == 0 else (OFF[r], d)

    def bc_open(a, stage, r=0):
        for wi, way in enumerate((1, -1)):
            src = slot(a, *offset(stage, r, 0))
            i = stage * 4 + r
            send(src, src, xs_s.at[a, i, wi], xs_r.at[a, i, wi], along(a, stage, way))

    def bc_pass(a, stage, r=0):
        for wi, way in enumerate((1, -1)):
            i = stage * 4 + r
            place = offset(stage, r, -way)
            arrived(slot(a, *place), xs_s.at[a, i, wi], xs_r.at[a, i, wi], along(a, stage, way))
            piece = slot(a, *place, wi)
            send(piece, piece, xf_s.at[a, i, wi], xf_r.at[a, i, wi], along(a, stage, way))

    def bc_end(a, stage, r=0):
        for wi, way in enumerate((1, -1)):
            i = stage * 4 + r
            arrived(slot(a, *offset(stage, r, 2), wi), xf_s.at[a, i, wi], xf_r.at[a, i, wi], along(a, stage, way))

    def branch(when, what):
        mode[0] = "start"
        pl.when(when)(what)
        mode[0] = "start, note"

    def note(what):
        mode[0] = "note"
        what()
        mode[0] = "start, note"

    def open_w():
        for q in range(2):
            if "start" in mode[0]:
                own(6 * q)
                own(6 * q + 1)
            ring_open(0, q)

    def open_x():
        for a in range(2):
            bc_open(a, 0, 0)
            bc_open(a, 1, 0)

    def x_head():
        for a in range(2):
            bc_pass(a, 0)
            for r in (1, 2):
                bc_open(a, 1, r)
        for a in range(2):
            bc_pass(a, 1, 0)
        for a in range(2):
            bc_end(a, 0)
            bc_open(a, 1, 3)

    def x_tail():
        for r in (1, 2):
            for a in range(2):
                bc_pass(a, 1, r)

    for i in (2, 3, 0, 1, 6, 7):
        swap_open(i)
    bias[core] = b_in[...].reshape(1, 864)
    send(bias.at[core], bias.at[core], bias_s, bias_r, at(flip=True))

    branch(stays, open_w)
    swap_pass(2)
    swap_pass(0)
    swap_pass(6)
    for a in range(2):
        own(2 + a)
    open_x()
    branch(moves, open_w)
    note(open_w)
    acc[...] = jnp.zeros_like(acc)
    for n, table in enumerate((b_out, gate_mod, gate_tan)):
        for i in range(16):
            first_row, lane = i * 320 // 128, i * 320 % 128
            flat = jnp.concatenate([table[first_row + j : first_row + j + 1, :] for j in range(3)], axis=1)
            gates[i, n : n + 1] = flat[:, lane : lane + 320]
    ring_step(0, 1)
    x_head()
    ring_step(0, 2)
    x_tail()
    for i in (4, 5):
        swap_open(i)
    for a in range(2):
        bc_pass(a, 1, 3)
    swap_pass(4)
    ring_step(0, 3)
    for q in range(2):
        own(4 + q)
        ring_open(1, q)
    for r in range(4):
        for a in range(2):
            bc_end(a, 1, r)

    def first(i, carry):
        delta = lax.rem(i + 6, 8)
        w = wbuf[0, delta].reshape(640, 864)
        for a in range(2):
            xk = xbuf[lax.rem(z + delta, 8), a].reshape(640, 256)
            acc[a] += lax.dot_general(xk, w, (((0,), (0,)), ((), ())), preferred_element_type=jnp.float32)
        return carry

    for delta in ORDER[:5]:
        sib_wait(0, delta)
    lax.fori_loop(0, 5, first, 0)
    ring_step(0, 4)
    for delta in ORDER[5:]:
        sib_wait(0, delta)
    lax.fori_loop(5, 8, first, 0)
    ring_step(1, 1)
    arrived(bias.at[1 - core], bias_s, bias_r, at(flip=True))

    def activate(i, carry):
        r = pl.ds(pl.multiple_of(i * 32, 32), 32)
        into = pl.ds(pl.multiple_of(lax.rem(i, 4) * 32, 32), 32)
        value, slope = gelu_pair(acc[0, r, :] + bias[y_hi])
        hid[i // 4, 0, into, :] = value.astype(jnp.bfloat16)
        hid[i // 4, 1, into, :] = (slope * acc[1, r, :]).astype(jnp.bfloat16)
        return carry

    lax.fori_loop(0, 8, activate, 0)

    def second(i):
        delta = ORDER[i]

        def body(h, carry):
            both = lax.dot_general(
                hid[...].reshape(512, 864), wbuf[1, delta, h], (((1,), (1,)), ((), ())),
                preferred_element_type=jnp.float32,
            )
            for yl in range(2):
                packed = jnp.concatenate(
                    [both[yl * 256 : yl * 256 + 128], both[yl * 256 + 128 : yl * 256 + 256]], axis=1
                ).astype(jnp.bfloat16)
                for b in range(4):
                    part[i, 0, b, h * 2 + yl] = packed[b * 32 : b * 32 + 16]
                    part[i, 1, h * 2 + yl, b] = packed[b * 32 + 16 : b * 32 + 32]
            return carry

        lax.fori_loop(0, 2, body, 0)
        for a in range(2):
            for wi, way in enumerate((1, -1)):
                send(
                    part.at[i, a, there(a, 2), pl.ds(2 * wi, 2)], r0.at[i, a, wi],
                    rs0_s.at[i, a, wi], rs0_r.at[i, a, wi], along(a, 0, way),
                )

    f32 = lambda v: v.astype(jnp.float32)

    def there(a, d):
        return lax.rem((x if a == 0 else y) + d + 4, 4)

    def reduce_zero(i):
        for a in range(2):
            for wi, way in enumerate((1, -1)):
                arrived(r0.at[i, a, wi], rs0_s.at[i, a, wi], rs0_r.at[i, a, wi], along(a, 0, way))
                j = there(a, way)
                for b in range(2):
                    t = f32(part[i, a, j, 2 * wi + b]) + f32(r0[i, a, wi, b])
                    part[i, a, j, 2 * wi + b] = t.astype(jnp.bfloat16)
                send(part.at[i, a, j], r1.at[i, a, wi], rs1_s.at[i, a, wi], rs1_r.at[i, a, wi], along(a, 0, way))

    def reduce_one(i):
        for a in range(2):
            for wi, way in enumerate((1, -1)):
                arrived(r1.at[i, a, wi], rs1_s.at[i, a, wi], rs1_r.at[i, a, wi], along(a, 0, way))
            for b in range(4):
                t = f32(part[i, a, there(a, 0), b]) + f32(r1[i, a, 0, b]) + f32(r1[i, a, 1, b])
                s2[i, a, b] = t.astype(jnp.bfloat16)
            for d in (2, 1, 3):
                send(
                    s2.at[i, a, there(1 - a, d)], r2.at[i, a, d - 1],
                    rs2_s.at[i, a, d - 1], rs2_r.at[i, a, d - 1], along(a, 1, d),
                )

    def reduce_two(i):
        delta = ORDER[i]
        g = gates[y_hi * 8 + lax.rem(z + delta, 8)]
        for d in (1, 2, 3):
            for a in range(2):
                arrived(r2.at[i, a, d - 1], rs2_s.at[i, a, d - 1], rs2_r.at[i, a, d - 1], along(a, 1, d))
        for cc in range(2):
            t = f32(s2[i, cc, there(1 - cc, 0)])
            for d in range(3):
                t += f32(r2[i, cc, d])
            shifted = t[:, :320] + g[0:1]
            fin[i, cc, 0] = (g[1:2] * shifted).astype(jnp.bfloat16)
            fin[i, cc, 1] = (g[1:2] * t[:, 320:] + g[2:3] * shifted).astype(jnp.bfloat16)
        if i:
            send(fin.at[i, core], land.at[i, 0], fin_s.at[i, 0], fin_r.at[i, 0], at(dz=delta))
        send(fin.at[i, 1 - core], land.at[i, 1], fin_s.at[i, 1], fin_r.at[i, 1], at(dz=delta, flip=True))

    def each(what, *items):
        for i in items:
            what(i)

    def block(i):
        sib_wait(1, ORDER[i])
        second(i)

    block(0)
    block(1)
    reduce_zero(0)
    block(2)
    reduce_one(0)
    each(reduce_zero, 1, 2)
    ring_step(1, 2)
    block(3)
    reduce_one(1)
    block(4)
    reduce_one(2)
    reduce_two(0)
    each(reduce_zero, 3, 4)
    ring_step(1, 3)
    block(5)
    reduce_one(3)
    block(6)
    reduce_one(4)
    each(reduce_two, 1, 2)
    each(reduce_zero, 5, 6)
    ring_step(1, 4)
    block(7)
    each(reduce_one, 5, 6)
    reduce_zero(7)
    each(reduce_two, 3, 4, 5, 6)
    reduce_one(7)
    reduce_two(7)

    for i in range(8):
        delta = ORDER[i]
        zz = lax.rem(z - delta + 8, 8)
        for other in range(2):
            cc = 1 - core if other else core
            if i or other:
                arrived(land.at[i, other], fin_s.at[i, other], fin_r.at[i, other], at(dz=-delta, flip=bool(other)))
                src = land[i, other]
            else:
                src = fin[i, core]
            out[0, cc * 8 + zz] = src[0]
            out[1, cc * 8 + zz] = src[1]

    @pl.when(moves)
    def _():
        for i in range(8):
            swap_copy(i).wait_send()

    for e in range(2):
        @pl.when(passes[e])
        def _():
            for i in (0, 2, 4, 6):
                relay_copy(i + e).wait_send()

    for c in sends:
        copy(*c).wait_send()


def part_ways(both, out_p, out_t):
    out_p[...] = both[0]
    out_t[...] = both[1]


def shards(primal, tangent, w_in, b_in, w_out, b_out, gate_mod, gate_tan):
    tables = [t.reshape(40, 128) for t in (b_out, gate_mod, gate_tan)]
    bf, dma = jnp.bfloat16, pltpu.SemaphoreType.DMA
    both = lambda *shape: [dma(shape), dma(shape)]
    both_out = pl.pallas_call(
        kernel,
        out_shape=jax.ShapeDtypeStruct((2, 16, 16, 320), bf),
        in_specs=[pl.BlockSpec(memory_space=pltpu.VMEM)] * 8,
        out_specs=pl.BlockSpec(memory_space=pltpu.VMEM),
        scratch_shapes=[
            pltpu.VMEM((2, 8, 2, 320, 864), bf),
            pltpu.VMEM((8, 2, 2, 320, 256), bf),
            pltpu.VMEM((2, 160, 864), bf),
            pltpu.VMEM((320, 256), bf),
            pltpu.VMEM((2, 1, 864), jnp.float32),
            pltpu.VMEM((16, 3, 320), jnp.float32),
            pltpu.VMEM((2, 256, 864), jnp.float32),
            pltpu.VMEM((2, 2, 128, 864), bf),
            pltpu.VMEM((8, 2, 4, 4, 16, 640), bf),
            pltpu.VMEM((8, 2, 2, 2, 16, 640), bf),
            pltpu.VMEM((8, 2, 2, 4, 16, 640), bf),
            pltpu.VMEM((8, 2, 4, 16, 640), bf),
            pltpu.VMEM((8, 2, 3, 16, 640), bf),
            pltpu.VMEM((8, 2, 2, 16, 320), bf),
            pltpu.VMEM((8, 2, 2, 16, 320), bf),
            *both(8), *both(8), dma, dma, *both(2, 2, 2, 4), *both(2, 2, 8),
            *both(2, 8, 2), *both(2, 8, 2), *both(8, 2, 2), *both(8, 2, 2), *both(8, 2, 3), *both(8, 2),
        ],
        compiler_params=pltpu.CompilerParams(
            collective_id=0, has_side_effects=True, vmem_limit_bytes=56 << 20
        ),
        cost_estimate=pl.CostEstimate(flops=9 * 10**9, bytes_accessed=3 * 10**6, transcendentals=221184),
        name="ffn_pair",
    )(primal.T, tangent.T, w_in, w_out.T, b_in, *tables)
    return pl.pallas_call(
        part_ways,
        out_shape=[jax.ShapeDtypeStruct((16, 16, 320), bf)] * 2,
        in_specs=[pl.BlockSpec(memory_space=pltpu.VMEM)],
        out_specs=[pl.BlockSpec(memory_space=pltpu.VMEM)] * 2,
        name="part_ways",
    )(both_out)


def solution(mesh):
    return jax.shard_map(
        shards,
        mesh=mesh,
        in_specs=(
            P("seq", "fsdp"),
            P("seq", "fsdp"),
            P("seq", "fsdp"),
            P("fsdp"),
            P("fsdp", "seq"),
            P(),
            P(),
            P(),
        ),
        out_specs=(P(None, "fsdp", "seq"), P(None, "fsdp", "seq")),
        check_vma=False,
    )
```
